32 devices in a mesh: dp: 8 (over z, y), shard: 4 (over x, core).
Axes of the slice: x: 2, y: 2, z: 4, core: 2. Of those that a mesh axis runs over, the one named last changes fastest.
Arguments:
- hidden: bfloat16 [64, 512, 768], P(('dp', 'shard')), may hold values from -6 to 6
- pair_lengths: int32 [64, 8], P(('dp', 'shard')), may hold values from 1 to 128, 512 in all within a row
- cotangent: bfloat16 [64, 512, 768], P(('dp', 'shard')), may hold values from -6 to 6
- query_weight: bfloat16 [768, 768], P(('dp', 'shard')), may hold values from -0.21875 to 0.21875
- query_bias: bfloat16 [768], P(('dp', 'shard')), may hold values from -3 to 3
- key_weight: bfloat16 [768, 768], P(('dp', 'shard')), may hold values from -0.21875 to 0.21875
- value_weight: bfloat16 [768, 768], P(('dp', 'shard')), may hold values from -0.21875 to 0.21875
- value_bias: bfloat16 [768], P(('dp', 'shard')), may hold values from -3 to 3
- out_weight: bfloat16 [768, 768], P(('dp', 'shard')), may hold values from -1.25 to 1.25
- out_bias: bfloat16 [768], P(('dp', 'shard')), may hold values from -3 to 3
- attn_gain: bfloat16 [768], P(('dp', 'shard')), may hold values from 0.099609375 to 1.8984375
- attn_shift: bfloat16 [768], P(('dp', 'shard')), may hold values from -3 to 3
- up_weight: bfloat16 [768, 3072], P(('dp', 'shard')), may hold values from -0.21875 to 0.21875
- up_bias: bfloat16 [3072], P(('dp', 'shard')), may hold values from -3 to 3
- down_weight: bfloat16 [3072, 768], P(('dp', 'shard')), may hold values from -0.109375 to 0.109375
- down_bias: bfloat16 [768], P(('dp', 'shard')), may hold values from -3 to 3
- final_gain: bfloat16 [768], P(('dp', 'shard')), may hold values from 0.099609375 to 1.8984375
- final_shift: bfloat16 [768], P(('dp', 'shard')), may hold values from -3 to 3
Outputs:
- layer_out: bfloat16 [64, 512, 768], P(('dp', 'shard'))
- grad_hidden: float32 [64, 512, 768], P(('dp', 'shard'))
- grad_query_weight: float32 [768, 768], P(('dp', 'shard'))
- grad_query_bias: float32 [768], P(('dp', 'shard'))
- grad_key_weight: float32 [768, 768], P(('dp', 'shard'))
- grad_value_weight: float32 [768, 768], P(('dp', 'shard'))
- grad_value_bias: float32 [768], P(('dp', 'shard'))
- grad_out_weight: float32 [768, 768], P(('dp', 'shard'))
- grad_out_bias: float32 [768], P(('dp', 'shard'))
- grad_attn_gain: float32 [768], P(('dp', 'shard'))
- grad_attn_shift: float32 [768], P(('dp', 'shard'))
- grad_up_weight: float32 [768, 3072], P(('dp', 'shard'))
- grad_up_bias: float32 [3072], P(('dp', 'shard'))
- grad_down_weight: float32 [3072, 768], P(('dp', 'shard'))
- grad_down_bias: float32 [768], P(('dp', 'shard'))
- grad_final_gain: float32 [768], P(('dp', 'shard'))
- grad_final_shift: float32 [768], P(('dp', 'shard'))
The draws below stay inside these ranges and needn't reach their ends.
Inputs may be any that keep to these rules, and one draw needn't show every extreme that they name: `pair_lengths`: the 8 pair lengths of a row sum to 512, and every row has a pair of exactly 128 tokens.
All inputs are finite; a program needn't handle non-finite values.
Results may differ from the reference program's by a relative error of at most 0.013.
Values may be sent and summed in bfloat16 or wider, within the bound.
No kernel may reach another device: no remote copies, remote signals or barrier semaphores. Data moves between devices by JAX's collectives and lax.ppermute only.
A program may use at most 192 MiB of HBM per device.

```python
import math
import jax
import jax.numpy as jnp
import numpy as np
from jax import lax

D = 768
HEADS = 12
FF = 3072
LEN = 512
PAIRS = 8
MOST = 128
ROWS = 64


def raised(values, own_key, source, target, blocks, factor):
    owner, partner = [(jnp.arange(values.shape[position]) // (values.shape[position] // blocks)).reshape([-1 if axis == position else 1 for axis in range(values.ndim)]) for position in (source, target)]
    chosen = jax.random.permutation(own_key, blocks)[partner]
    strong = (owner == chosen) | (owner == (partner + blocks // 2) % blocks)
    return jnp.where(strong, factor * values, values)


def shard_levels(rng, dims, pieces, low, top_value):
    loudness, own = 1.0, jax.random.fold_in(rng, 6)
    for dim, blocks in pieces:
        heights = jnp.exp(jax.random.uniform(jax.random.fold_in(own, dim), (blocks,), jnp.float32, low / len(pieces), top_value / len(pieces)))
        loudness = loudness * jnp.repeat(heights, dims[dim] // blocks).reshape([-1 if axis == dim else 1 for axis in range(len(dims))])
    return loudness


def profile(number_of, total, most, lean):
    portions = [(1 << 20) // math.isqrt(grade ** lean) + 1 for grade in range(2, number_of + 1)]
    rest, given = total - most - (number_of - 1), [1] * (number_of - 1)
    while rest > 0:
        candidates = [i for i in range(number_of - 1) if given[i] < most]
        mass, left = sum([portions[i] for i in candidates]), rest
        for i in candidates:
            addition = min(most - given[i], max(1, left * portions[i] // mass), rest)
            given[i] = given[i] + addition
            rest = rest - addition
    return np.array([most] + given)


def ragged(key, number_of, total, bound, lean):
    if number_of == 2:
        one = jax.random.randint(key, (), max(1, total - bound), min(bound, total - 1) + 1)
        return jnp.stack([one, total - one])
    sizes = jnp.asarray(profile(number_of, total, bound, lean), jnp.int32)
    twos = (number_of - 1) // 2
    giver, sink = sizes[1:1 + 2 * twos:2], sizes[2:2 + 2 * twos:2]
    room = jnp.minimum(giver - 1, bound - sink)
    shifted = jax.random.randint(jax.random.fold_in(key, 1), (twos,), 0, 1 << 20) % (room + 1)
    sizes = sizes.at[1:1 + 2 * twos:2].set(giver - shifted).at[2:2 + 2 * twos:2].set(sink + shifted)
    return sizes[jax.random.permutation(jax.random.fold_in(key, 2), number_of)]


def bell_draw(own_key, shape, spread, most, cuts=(), kind=jnp.bfloat16):
    values = jax.random.normal(own_key, shape, jnp.float32) * spread
    if len(cuts) > 0:
        values = shard_levels(own_key, shape, cuts, -0.22, 0.18) * values
    return jnp.clip(values, min=-most, max=most).astype(kind)


def heavy_noise(own_key, extent, deviation, bound, shards, heavy, kind=jnp.bfloat16):
    entries = deviation * jax.random.normal(own_key, extent, jnp.float32)
    if shards:
        entries = entries * shard_levels(own_key, extent, shards, -0.22, 0.18)
    return jnp.clip(raised(entries, jax.random.fold_in(own_key, 3), *heavy), -bound, bound).astype(kind)


def setup_inputs(seed: int = 0) -> dict:
    keys = jax.random.split(jax.random.key(seed), 19)
    hidden = bell_draw(keys[0], (ROWS, LEN, D), 1.0, 6.0, ((0, 32),))
    pair_lengths = jax.vmap(lambda own: ragged(own, PAIRS, LEN, MOST, 2))(jax.random.split(keys[1], ROWS)).reshape((ROWS, PAIRS)).astype(jnp.int32)
    cotangent = heavy_noise(keys[2], (ROWS, LEN, D), 1.0, 6.0, ((0, 32),), (0, 2, 32, 2.75))
    query_weight = bell_draw(keys[3], (D, D), D ** -0.5, 0.21875, ((0, 32),))
    query_bias = bell_draw(keys[4], (D,), 0.5, 3.0, ((0, 32),))
    key_weight = bell_draw(keys[5], (D, D), D ** -0.5, 0.21875, ((0, 32),))
    value_weight = bell_draw(keys[6], (D, D), D ** -0.5, 0.21875, ((0, 32),))
    value_bias = bell_draw(keys[7], (D,), 0.5, 3.0, ((0, 32),))
    out_weight = bell_draw(keys[8], (D, D), (D // 32) ** -0.5, 1.25, ((0, 32),))
    out_bias = bell_draw(keys[9], (D,), 0.5, 3.0, ((0, 32),))
    attn_gain = jnp.clip(1.0 + 0.18 * jax.random.normal(keys[10], (D,), jnp.float32), 0.099609375, 1.8984375).astype(jnp.bfloat16)
    attn_shift = bell_draw(keys[11], (D,), 0.5, 3.0, ((0, 32),))
    up_weight = bell_draw(keys[12], (D, FF), D ** -0.5, 0.21875, ((0, 32),))
    up_bias = bell_draw(keys[13], (FF,), 0.5, 3.0, ((0, 32),))
    down_weight = bell_draw(keys[14], (FF, D), FF ** -0.5, 0.109375, ((0, 32),))
    down_bias = bell_draw(keys[15], (D,), 0.5, 3.0, ((0, 32),))
    final_gain = jnp.clip(1.0 + 0.18 * jax.random.normal(keys[16], (D,), jnp.float32), 0.099609375, 1.8984375).astype(jnp.bfloat16)
    final_shift = bell_draw(keys[17], (D,), 0.5, 3.0, ((0, 32),))
    return dict(hidden=hidden, pair_lengths=pair_lengths, cotangent=cotangent, query_weight=query_weight, query_bias=query_bias, key_weight=key_weight, value_weight=value_weight, value_bias=value_bias, out_weight=out_weight, out_bias=out_bias, attn_gain=attn_gain, attn_shift=attn_shift, up_weight=up_weight, up_bias=up_bias, down_weight=down_weight, down_bias=down_bias, final_gain=final_gain, final_shift=final_shift)


EPSILON = 1e-06
SQRT_HALF = 0.7071067811865476
score_scale = 0.125
HIGH = lax.Precision.HIGHEST

@jax.custom_vjp
def low(v):
    return lax.optimization_barrier(v.astype(jnp.bfloat16)).astype(jnp.float32)

@jax.custom_vjp
def low_back(v):
    return v

def low_keep(v):
    return (low(v), None)

def low_pass(kept, grad):
    return (grad,)

def back_keep(v):
    return (v, None)

def back_low(kept, grad):
    return (low(grad),)
low.defvjp(low_keep, low_pass)
low_back.defvjp(back_keep, back_low)

def rounded_both(value):
    return low(low_back(value))

def matmul(left, right):
    return jnp.dot(left, right, precision=HIGH)

def layer_norm(rows, gain, shift):
    centred = rows - lax.optimization_barrier(jnp.mean(rows, -1, keepdims=True))
    inverse = lax.rsqrt(lax.optimization_barrier(jnp.mean(centred * centred, -1, keepdims=True)) + EPSILON)
    return centred * inverse * gain + shift

def doc_mask(pair_lens, size):
    pair_ends = jnp.cumsum(pair_lens)
    positions = jnp.arange(size, dtype=jnp.int32)
    doc_index = lax.optimization_barrier(jnp.sum((positions[:, None] >= pair_ends[None, :]).astype(jnp.int32), -1))
    return doc_index[:, None] == doc_index[None, :]

def forward(params, tokens, same_pair):
    query_mat, query_add, key_mat, value_mat, value_add, out_mat, out_add, first_gain, first_shift, up_mat, up_add, down_mat, down_add, second_gain, second_shift = params
    length = tokens.shape[0]
    queries = rounded_both(matmul(tokens, query_mat) + query_add).reshape(length, HEADS, -1)
    keys_all = rounded_both(matmul(tokens, key_mat)).reshape(length, HEADS, -1)
    values_all = rounded_both(matmul(tokens, value_mat) + value_add).reshape(length, HEADS, -1)
    scores = jnp.einsum('qhd,khd->hqk', queries, keys_all, precision=HIGH) * score_scale
    scores = low_back(jnp.where(same_pair[None], scores, -1e+30))
    row_max = lax.optimization_barrier(jnp.max(scores, -1, keepdims=True))
    exp_scores = jnp.exp(scores - row_max)
    attn_probs = exp_scores / lax.optimization_barrier(jnp.sum(exp_scores, -1, keepdims=True))
    mixed = jnp.einsum('hqk,khd->qhd', low(attn_probs), values_all, precision=HIGH)
    mixed = rounded_both(mixed.reshape(length, -1))
    first_sum = tokens + low_back(matmul(mixed, out_mat) + out_add)
    middle = layer_norm(first_sum, first_gain, first_shift)
    pre_act = low_back(matmul(low(middle), up_mat) + up_add)
    activated = low(pre_act * 0.5 * (1.0 + lax.erf(pre_act * SQRT_HALF)))
    second_sum = middle + low_back(matmul(activated, down_mat) + down_add)
    return layer_norm(second_sum, second_gain, second_shift)

def reference(hidden, pair_lengths, cotangent, query_weight, query_bias, key_weight, value_weight, value_bias, out_weight, out_bias, attn_gain, attn_shift, up_weight, up_bias, down_weight, down_bias, final_gain, final_shift):
    params = tuple((weight.astype(jnp.float32) for weight in (query_weight, query_bias, key_weight, value_weight, value_bias, out_weight, out_bias, attn_gain, attn_shift, up_weight, up_bias, down_weight, down_bias, final_gain, final_shift)))

    def one_row(totals, packed):
        row_tokens, pair_lens, row_grad = packed
        same_pair = doc_mask(pair_lens, row_tokens.shape[0])
        result, pullback = jax.vjp(lambda prm, toks: forward(prm, toks, same_pair), params, row_tokens.astype(jnp.float32))
        grad_params, grad_tokens = pullback(row_grad.astype(jnp.float32))
        totals = tuple((total + grad for total, grad in zip(totals, grad_params)))
        return (totals, (result.astype(jnp.bfloat16), grad_tokens))
    zeros = tuple((jnp.zeros(weight.shape, jnp.float32) for weight in params))
    grads, (layer_out, grad_hidden) = lax.scan(one_row, zeros, (hidden, pair_lengths, cotangent))
    return (layer_out, grad_hidden, grads[0], grads[1], grads[2], grads[3], grads[4], grads[5], grads[6], grads[7], grads[8], grads[9], grads[10], grads[11], grads[12], grads[13], grads[14])
```

```python
import jax
import jax.numpy as jnp
from jax import lax
from jax.sharding import PartitionSpec as P

HEADS = 12


EPSILON = 1e-06
SQRT_HALF = 0.7071067811865476
INV_ROOT = 0.3989422804014327
score_scale = 0.125

AXES = ("dp", "shard")
f32 = jnp.float32
bf16 = jnp.bfloat16
cat = jnp.concatenate


def moves(move):
    pairs = []
    for index in range(32):
        z, y, x, core = index // 8, (index // 4) % 2, (index // 2) % 2, index % 2
        z, y, x, core = move(z, y, x, core)
        pairs.append((index, z * 8 + y * 4 + x * 2 + core))
    return pairs


MOVES = {
    "core": moves(lambda z, y, x, core: (z, y, x, 1 - core)),
    "x": moves(lambda z, y, x, core: (z, y, 1 - x, core)),
    "y": moves(lambda z, y, x, core: (z, 1 - y, x, core)),
    "z1": moves(lambda z, y, x, core: ((z + 1) % 4, y, x, core)),
    "z2": moves(lambda z, y, x, core: ((z + 2) % 4, y, x, core)),
    "z3": moves(lambda z, y, x, core: ((z + 3) % 4, y, x, core)),
}


def send(values, move):
    return lax.ppermute(values, AXES, MOVES[move])


def place():
    major, minor = lax.axis_index("dp"), lax.axis_index("shard")
    return major // 2, major % 2, minor // 2, minor % 2


def phase(*values):
    return lax.optimization_barrier(values)


def add(*terms):
    total = terms[0].astype(f32)
    for term in terms[1:]:
        total = total + term.astype(f32)
    return total


def gather_blocks(block, split):
    z, y, x, core = place()
    one, two, three = send(block, "z1"), send(block, "z2"), send(block, "z3")
    one, two, three = phase(one, two, three)
    line = jnp.stack([block, one, two, three])
    first, second = line[:, :split], line[:, split:]
    first_x, second_y = send(first, "x"), send(second, "y")
    first_x, second_y, first, second = phase(first_x, second_y, first, second)
    first, second = cat([first, first_x]), cat([second, second_y])
    first_y, second_x = send(first, "y"), send(second, "x")
    other_first, other_second = send(first, "core"), send(second, "core")
    first, first_y, second, second_x, other_first, other_second = phase(
        first, first_y, second, second_x, other_first, other_second
    )
    other_first_y, other_second_x = send(first_y, "core"), send(second_x, "core")
    halves = []
    for a, b, c, d in (
        (first, first_y, second, second_x),
        (other_first, other_first_y, other_second, other_second_x),
    ):
        first_all = cat([a, b]).reshape(2, 2, 4, *first.shape[1:])
        second_all = cat([c, d]).reshape(2, 2, 4, *second.shape[1:]).swapaxes(0, 1)
        halves.append(cat([first_all, second_all], 3).reshape(16, *block.shape))
    chips = jnp.arange(16)
    source = ((chips // 2 % 2) ^ y) * 8 + ((chips % 2) ^ x) * 4 + (z - chips // 4) % 4
    return halves[0][source], halves[1][source]


def scatter_blocks(blocks, split):
    z, y, x, core = place()
    half = blocks.shape[2] // 2
    keep = lax.dynamic_slice_in_dim(blocks, core * half, half, 2)
    away = lax.dynamic_slice_in_dim(blocks, (1 - core) * half, half, 2).astype(bf16)
    (got,) = phase(send(away, "core"))
    summed = add(keep, got).astype(bf16).reshape(4, 2, 2, *blocks.shape[1:2], half)
    pick = lax.dynamic_index_in_dim
    first, second = summed[:, :, :, :split], summed[:, :, :, split:]
    got_first = send(pick(first, 1 - y, 1, False), "y")
    got_second = send(pick(second, 1 - x, 2, False), "x")
    got_first, got_second, first, second = phase(got_first, got_second, first, second)
    first = add(pick(first, y, 1, False), got_first).astype(bf16)
    second = add(pick(second, x, 2, False), got_second).astype(bf16)
    got_first = send(pick(first, 1 - x, 1, False), "x")
    got_second = send(pick(second, 1 - y, 1, False), "y")
    got_first, got_second, first, second = phase(got_first, got_second, first, second)
    first = add(pick(first, x, 1, False), got_first)
    second = add(pick(second, y, 1, False), got_second)
    line = cat([first, second], 1)
    low = line.astype(bf16)
    one = send(pick(low, (z + 1) % 4, 0, False), "z1")
    two = send(pick(low, (z + 2) % 4, 0, False), "z2")
    three = send(pick(low, (z + 3) % 4, 0, False), "z3")
    one, two, three, line = phase(one, two, three, line)
    return add(pick(line, z, 0, False), one, two, three)


def gather_attention(matrices, vector):
    z, y, x, core = place()
    count, rows, width = matrices.shape
    half = width // 2
    mine = lax.dynamic_slice_in_dim(matrices, core * half, half, 2)
    got = send(lax.dynamic_slice_in_dim(matrices, (1 - core) * half, half, 2), "core")
    pair = jnp.where(core == 0, cat([mine, got], 1), cat([got, mine], 1))
    vector_rows = jnp.pad(vector[None], ((0, 15), (0, half - vector.shape[0])))
    block = cat([pair.reshape(count * 2 * rows, half), vector_rows])
    (block,) = phase(block)
    own, other = gather_blocks(block, count * rows)
    full = jnp.where(core == 0, cat([own, other], 2), cat([other, own], 2))
    size = count * 2 * rows
    mats = full[:, :size].reshape(16, count, 2 * rows, width).swapaxes(0, 1).reshape(count, 16 * 2 * rows, width)
    entries = vector.shape[0]
    vectors = full[:, size].reshape(32, half)[:, :entries]
    return mats, vectors


def scatter_attention(matrices, vectors):
    z, y, x, core = place()
    count, full_rows, width = matrices.shape
    half = width // 2
    rows = full_rows // 32
    blocks = matrices.reshape(count, 16, 2 * rows, width).swapaxes(0, 1).reshape(16, count * 2 * rows, width)
    entries = vectors.shape[1]
    vector_rows = jnp.pad(vectors, ((0, 0), (0, half - entries))).reshape(16, 1, width)
    vector_rows = jnp.pad(vector_rows, ((0, 0), (0, 15), (0, 0)))
    line = scatter_blocks(cat([blocks, vector_rows], 1), count * rows)
    size = count * 2 * rows
    mine = line[:size].reshape(count, 2, rows, half)
    keep = lax.dynamic_index_in_dim(mine, core, 1, False)
    got = send(lax.dynamic_index_in_dim(mine, 1 - core, 1, False).astype(bf16), "core").astype(f32)
    whole = jnp.where(core == 0, cat([keep, got], 2), cat([got, keep], 2))
    return whole, line[size, :entries]


def gather_attention_any(matrices, vector):
    mats = lax.all_gather(matrices, AXES, axis=1, tiled=True)
    return mats, lax.all_gather(vector, AXES, axis=0, tiled=False)


def scatter_attention_any(matrices, vectors):
    mats = lax.psum_scatter(matrices.astype(bf16), AXES, scatter_dimension=1, tiled=True)
    return mats.astype(f32), lax.psum_scatter(vectors, AXES, scatter_dimension=0, tiled=False)


def matmul(left, right):
    return jnp.dot(left, right, preferred_element_type=jnp.float32)


def outer_sum(left, right):
    return jnp.einsum("ta,tb->ab", left, right, preferred_element_type=jnp.float32)


def back_product(grads, weights):
    return jnp.einsum("tb,ab->ta", grads, weights, preferred_element_type=jnp.float32)


def normalize(rows):
    centred = rows - jnp.mean(rows, -1, keepdims=True)
    inverse = lax.rsqrt(jnp.mean(centred * centred, -1, keepdims=True) + EPSILON)
    return (centred * inverse, inverse)


def norm_back(grad_rows, normed, inverse, gain):
    grad_norm = grad_rows * gain
    return inverse * (
        grad_norm
        - jnp.mean(grad_norm, -1, keepdims=True)
        - normed * jnp.mean(grad_norm * normed, -1, keepdims=True)
    )


def doc_mask(pair_lens, size):
    pair_ends = jnp.cumsum(pair_lens)
    positions = jnp.arange(size, dtype=jnp.int32)
    doc_index = jnp.sum((positions[:, None] >= pair_ends[None, :]).astype(jnp.int32), -1)
    return doc_index[:, None] == doc_index[None, :]


def split_heads(rows):
    return rows.reshape(rows.shape[0], HEADS, rows.shape[1] // HEADS)


def scores_of(query_heads, key_heads, pair_lens):
    scores = (
        jnp.einsum("qhd,khd->hqk", query_heads, key_heads, preferred_element_type=jnp.float32)
        * score_scale
    )
    return jnp.where(doc_mask(pair_lens, query_heads.shape[0])[None], scores, -1e30)


def attend(packed):
    query_rows, key_rows, value_rows, pair_lens = packed
    scores = scores_of(split_heads(query_rows), split_heads(key_rows), pair_lens)
    row_max = jnp.max(scores, -1, keepdims=True)
    exp_scores = jnp.exp(scores - row_max)
    totals = jnp.sum(exp_scores, -1, keepdims=True)
    attn_probs = exp_scores / totals
    mixed = jnp.einsum(
        "hqk,khd->qhd",
        attn_probs.astype(jnp.bfloat16),
        split_heads(value_rows),
        preferred_element_type=jnp.float32,
    )
    log_total = (row_max + jnp.log(totals))[..., 0]
    return (mixed.reshape(query_rows.shape).astype(jnp.bfloat16), log_total)


def attend_back(packed):
    query_rows, key_rows, value_rows, pair_lens, log_total, grad_rows = packed
    query_heads = split_heads(query_rows)
    key_heads = split_heads(key_rows)
    grad_heads = split_heads(grad_rows)
    scores = scores_of(query_heads, key_heads, pair_lens)
    attn_probs = jnp.exp(scores - log_total[..., None])
    grad_values = jnp.einsum(
        "hqk,qhd->khd",
        attn_probs.astype(jnp.bfloat16),
        grad_heads,
        preferred_element_type=jnp.float32,
    )
    grad_probs = jnp.einsum(
        "qhd,khd->hqk", grad_heads, split_heads(value_rows), preferred_element_type=jnp.float32
    )
    centre = jnp.sum(grad_probs * attn_probs, -1, keepdims=True)
    grad_scores = (attn_probs * (grad_probs - centre)).astype(jnp.bfloat16)
    grad_queries = (
        jnp.einsum("hqk,khd->qhd", grad_scores, key_heads, preferred_element_type=jnp.float32)
        * score_scale
    )
    grad_keys = (
        jnp.einsum("hqk,qhd->khd", grad_scores, query_heads, preferred_element_type=jnp.float32)
        * score_scale
    )
    row_shape = query_rows.shape
    return (
        grad_queries.reshape(row_shape).astype(jnp.bfloat16),
        grad_keys.reshape(row_shape).astype(jnp.bfloat16),
        grad_values.reshape(row_shape).astype(jnp.bfloat16),
    )


def per_device(
    known,
    hidden,
    pair_lengths,
    cotangent,
    query_weight,
    query_bias,
    key_weight,
    value_weight,
    value_bias,
    out_weight,
    out_bias,
    attn_gain,
    attn_shift,
    up_weight,
    up_bias,
    down_weight,
    down_bias,
    final_gain,
    final_shift,
):
    rows_here, length, width = hidden.shape
    count = rows_here * length
    share = query_weight.shape[0]
    devices = width // share
    chunks = up_weight.shape[1] // width
    up_mine = (
        up_weight.reshape(share, devices, chunks, share).swapaxes(1, 2).reshape(share, chunks * width)
    )
    down_mine = down_weight.reshape(chunks, share, width).swapaxes(0, 1).reshape(share, chunks * width)
    ffn_mine = cat([up_mine, down_mine], 1)
    ffn_full = lax.all_gather(ffn_mine, AXES, axis=0, tiled=True)
    vector = cat(
        [
            query_bias,
            value_bias,
            out_bias,
            attn_gain,
            attn_shift,
            down_bias,
            final_gain,
            final_shift,
            up_bias,
        ]
    )
    matrices = jnp.stack([query_weight, key_weight, value_weight, out_weight])
    mats, vectors = (gather_attention if known else gather_attention_any)(matrices, vector)
    query_mat, key_mat, value_mat, out_mat = mats[0], mats[1], mats[2], mats[3]
    vectors = (
        vectors.reshape(devices, 8 + chunks, share).swapaxes(0, 1).reshape(8 + chunks, width).astype(f32)
    )
    query_add, value_add, out_add, first_gain, first_shift, down_add, second_gain, second_shift = (
        vectors[i] for i in range(8)
    )
    up_add = vectors[8:].reshape(chunks * width)
    up_mat = ffn_full[:, : chunks * width]
    down_mat = ffn_full[:, chunks * width :].reshape(width, chunks, width)
    tokens = hidden.reshape(count, width)
    queries = (matmul(tokens, query_mat) + query_add).astype(jnp.bfloat16)
    keys_all = matmul(tokens, key_mat).astype(jnp.bfloat16)
    values_all = (matmul(tokens, value_mat) + value_add).astype(jnp.bfloat16)
    query_rows = queries.reshape(rows_here, length, width)
    key_rows = keys_all.reshape(rows_here, length, width)
    value_rows = values_all.reshape(rows_here, length, width)
    mixed_rows, log_totals = lax.map(attend, (query_rows, key_rows, value_rows, pair_lengths))
    mixed = mixed_rows.reshape(count, width)
    first_sum = tokens.astype(jnp.float32) + matmul(mixed, out_mat) + out_add
    first_norm, first_inverse = normalize(first_sum)
    middle = first_norm * first_gain + first_shift
    middle_low = middle.astype(jnp.bfloat16)
    pre_act = matmul(middle_low, up_mat) + up_add
    cdf_part = 0.5 * (1.0 + lax.erf(pre_act * SQRT_HALF))
    activated = (pre_act * cdf_part).astype(jnp.bfloat16)
    act_parts = activated.reshape(count, chunks, width)
    second_sum = (
        middle
        + jnp.einsum("tgi,ign->tn", act_parts, down_mat, preferred_element_type=jnp.float32)
        + down_add
    )
    second_norm, second_inverse = normalize(second_sum)
    layer_out = (second_norm * second_gain + second_shift).astype(jnp.bfloat16).reshape(hidden.shape)
    grad_out = cotangent.reshape(count, width).astype(jnp.float32)
    grad_final_gain = jnp.sum(grad_out * second_norm, 0)
    grad_final_shift = jnp.sum(grad_out, 0)
    grad_second = norm_back(grad_out, second_norm, second_inverse, second_gain)
    grad_second_low = grad_second.astype(jnp.bfloat16)
    grad_down_bias = jnp.sum(grad_second_low.astype(jnp.float32), 0)
    grad_down = jnp.einsum("tgi,tn->ign", act_parts, grad_second_low, preferred_element_type=f32)
    grad_act = jnp.einsum("tn,ign->tgi", grad_second_low, down_mat, preferred_element_type=f32)
    density = jnp.exp(-0.5 * pre_act * pre_act) * INV_ROOT
    grad_pre = (grad_act.reshape(pre_act.shape) * (cdf_part + pre_act * density)).astype(jnp.bfloat16)
    grad_up_bias = jnp.sum(grad_pre.astype(jnp.float32), 0)
    grad_up = outer_sum(middle_low, grad_pre)
    ffn_grads = cat([grad_up.astype(bf16), grad_down.astype(bf16).reshape(width, chunks * width)], 1)
    ffn_owned = lax.psum_scatter(ffn_grads, AXES, scatter_dimension=0, tiled=True).astype(f32)
    grad_middle = grad_second + back_product(grad_pre, up_mat)
    grad_attn_gain = jnp.sum(grad_middle * first_norm, 0)
    grad_attn_shift = jnp.sum(grad_middle, 0)
    grad_first = norm_back(grad_middle, first_norm, first_inverse, first_gain)
    grad_first_low = grad_first.astype(jnp.bfloat16)
    grad_out_bias = jnp.sum(grad_first_low.astype(jnp.float32), 0)
    grad_out_weight = outer_sum(mixed, grad_first_low)
    grad_mixed = back_product(grad_first_low, out_mat).astype(jnp.bfloat16)
    grad_query_rows, grad_key_rows, grad_value_rows = lax.map(
        attend_back,
        (
            query_rows,
            key_rows,
            value_rows,
            pair_lengths,
            log_totals,
            grad_mixed.reshape(rows_here, length, width),
        ),
    )
    grad_queries = grad_query_rows.reshape(count, width)
    grad_keys = grad_key_rows.reshape(count, width)
    grad_values = grad_value_rows.reshape(count, width)
    grad_query_bias = jnp.sum(grad_queries.astype(jnp.float32), 0)
    grad_value_bias = jnp.sum(grad_values.astype(jnp.float32), 0)
    mat_grads = jnp.stack(
        [
            outer_sum(tokens, grad_queries),
            outer_sum(tokens, grad_keys),
            outer_sum(tokens, grad_values),
            grad_out_weight,
        ]
    )
    grad_tokens = (
        grad_first
        + back_product(grad_queries, query_mat)
        + back_product(grad_keys, key_mat)
        + back_product(grad_values, value_mat)
    )
    vector_grads = jnp.stack(
        [
            grad_query_bias,
            grad_value_bias,
            grad_out_bias,
            grad_attn_gain,
            grad_attn_shift,
            grad_down_bias,
            grad_final_gain,
            grad_final_shift,
        ]
    )
    vector_grads = cat([vector_grads, grad_up_bias.reshape(chunks, width)])
    vector_grads = (
        vector_grads.reshape(8 + chunks, devices, share).swapaxes(0, 1).reshape(devices, (8 + chunks) * share)
    )
    mats_owned, vectors_owned = (scatter_attention if known else scatter_attention_any)(
        mat_grads, vector_grads
    )
    own = vectors_owned.reshape(8 + chunks, share)
    up_owned = (
        ffn_owned[:, : chunks * width]
        .reshape(share, chunks, devices, share)
        .swapaxes(1, 2)
        .reshape(share, chunks * width)
    )
    down_owned = (
        ffn_owned[:, chunks * width :].reshape(share, chunks, width).swapaxes(0, 1).reshape(chunks * share, width)
    )
    return (
        layer_out,
        grad_tokens.reshape(hidden.shape),
        mats_owned[0],
        own[0],
        mats_owned[1],
        mats_owned[2],
        own[1],
        mats_owned[3],
        own[2],
        own[3],
        own[4],
        up_owned,
        own[8:].reshape(chunks * share),
        down_owned,
        own[5],
        own[6],
        own[7],
    )


def solution(mesh):
    known = dict(mesh.shape) == {"dp": 8, "shard": 4}
    cube, flat, line = P(AXES, None, None), P(AXES, None), P(AXES)
    return jax.shard_map(
        lambda *args: per_device(known, *args),
        mesh=mesh,
        in_specs=(
            cube, flat, cube, flat, line, flat, flat, line, flat, line, line, line, flat, line, flat, line, line, line,
        ),
        out_specs=(
            cube, cube, flat, line, flat, flat, line, flat, line, line, line, flat, line, flat, line, line, line,
        ),
        check_vma=False,
    )
```

```python
import functools

import jax
import jax.numpy as jnp
from jax import lax
from jax.experimental import pallas as pl
from jax.experimental.pallas import tpu as pltpu
from jax.sharding import PartitionSpec as P

EPSILON = 1e-06
SQRT_HALF = 0.7071067811865476
INV_ROOT = 0.3989422804014327
MOST = 128
HALF = 64
NEVER = -1e30
MEGA = 1024 * 1024

AXES = ("dp", "shard")
f32 = jnp.float32
bf16 = jnp.bfloat16
cat = jnp.concatenate


def moves(move):
    pairs = []
    for index in range(32):
        z, y, x, core = index // 8, (index // 4) % 2, (index // 2) % 2, index % 2
        z, y, x, core = move(z, y, x, core)
        pairs.append((index, z * 8 + y * 4 + x * 2 + core))
    return pairs


MOVES = {
    "core": moves(lambda z, y, x, core: (z, y, x, 1 - core)),
    "x": moves(lambda z, y, x, core: (z, y, 1 - x, core)),
    "y": moves(lambda z, y, x, core: (z, 1 - y, x, core)),
    "z1": moves(lambda z, y, x, core: ((z + 1) % 4, y, x, core)),
    "z2": moves(lambda z, y, x, core: ((z + 2) % 4, y, x, core)),
    "z3": moves(lambda z, y, x, core: ((z + 3) % 4, y, x, core)),
}


def send(values, move):
    return lax.ppermute(values, AXES, MOVES[move])


def place():
    major, minor = lax.axis_index("dp"), lax.axis_index("shard")
    return major // 2, major % 2, minor // 2, minor % 2


def phase(*values):
    return lax.optimization_barrier(values)


def add(*terms):
    total = terms[0].astype(f32)
    for term in terms[1:]:
        total = total + term.astype(f32)
    return total


def gather_blocks(block, split):
    one, two, three = send(block, "z1"), send(block, "z2"), send(block, "z3")
    one, two, three = phase(one, two, three)
    line = jnp.stack([block, one, two, three])
    first, second = line[:, :split], line[:, split:]
    first_x, second_y = send(first, "x"), send(second, "y")
    first_x, second_y, first, second = phase(first_x, second_y, first, second)
    first, second = cat([first, first_x]), cat([second, second_y])
    first_y, second_x = send(first, "y"), send(second, "x")
    other_first, other_second = send(first, "core"), send(second, "core")
    first, first_y, second, second_x, other_first, other_second = phase(
        first, first_y, second, second_x, other_first, other_second
    )
    other_first_y, other_second_x = send(first_y, "core"), send(second_x, "core")
    return first, first_y, second, second_x, other_first, other_first_y, other_second, other_second_x


def scatter_blocks(keep, away, split):
    z, y, x, core = place()
    got, keep = phase(send(away, "core"), keep)
    shape = (4, 2, 2, *keep.shape[1:])
    keep, got = keep.reshape(shape), got.reshape(shape)

    def pick(values, index, axis):
        return lax.dynamic_index_in_dim(values, index, axis, False)

    def part(index, axis, rows):
        return add(pick(keep, index, axis)[:, :, rows], pick(got, index, axis)[:, :, rows]).astype(bf16)

    top, rest = slice(0, split), slice(split, None)
    got_first = send(part(1 - y, 1, top), "y")
    got_second = send(part(1 - x, 2, rest), "x")
    first, second = part(y, 1, top), part(x, 2, rest)
    got_first, got_second, first, second = phase(got_first, got_second, first, second)

    def both(one, two, index):
        return add(pick(one, index, 1), pick(two, index, 1)).astype(bf16)

    got_first_x = send(both(first, got_first, 1 - x), "x")
    got_second_y = send(both(second, got_second, 1 - y), "y")
    first, second = both(first, got_first, x), both(second, got_second, y)
    got_first_x, got_second_y, first, second = phase(got_first_x, got_second_y, first, second)
    line = cat([add(first, got_first_x), add(second, got_second_y)], 1)
    low = line.astype(bf16)
    one = send(pick(low, (z + 1) % 4, 0), "z1")
    two = send(pick(low, (z + 2) % 4, 0), "z2")
    three = send(pick(low, (z + 3) % 4, 0), "z3")
    mine = pick(line, z, 0)
    one, two, three, mine = phase(one, two, three, mine)
    return add(mine, one, two, three)


def gather_attention(matrices, vector):
    z, y, x, core = place()
    count, rows, width = matrices.shape
    half = width // 2
    mine = lax.dynamic_slice_in_dim(matrices, core * half, half, 2)
    got = send(lax.dynamic_slice_in_dim(matrices, (1 - core) * half, half, 2), "core")
    pair = jnp.where(core == 0, cat([mine, got], 1), cat([got, mine], 1))
    vector_rows = jnp.pad(vector[None], ((0, 15), (0, half - vector.shape[0])))
    block = cat([pair.reshape(count * 2 * rows, half), vector_rows])
    (block,) = phase(block)
    return gather_blocks(block, count * rows)


def scatter_attention(keep, away, count, rows, entries):
    z, y, x, core = place()
    half = keep.shape[2]
    line = scatter_blocks(keep, away, count * rows)
    size = count * 2 * rows
    mine = line[:size].reshape(count, 2, rows, half)
    kept = lax.dynamic_index_in_dim(mine, core, 1, False)
    got = send(lax.dynamic_index_in_dim(mine, 1 - core, 1, False).astype(bf16), "core").astype(f32)
    whole = jnp.where(core == 0, cat([kept, got], 2), cat([got, kept], 2))
    return whole, line[size, :entries]


def gather_attention_any(matrices, vector):
    mats = lax.all_gather(matrices, AXES, axis=1, tiled=True)
    return mats, lax.all_gather(vector, AXES, axis=0, tiled=False)


def scatter_attention_any(matrices, vectors):
    mats = lax.psum_scatter(matrices.astype(bf16), AXES, scatter_dimension=1, tiled=True)
    return mats.astype(f32), lax.psum_scatter(vectors, AXES, scatter_dimension=0, tiled=False)


def dot(left, right):
    return lax.dot_general(left, right, (((1,), (0,)), ((), ())), preferred_element_type=f32)


def dot_nt(left, right):
    return lax.dot_general(left, right, (((1,), (1,)), ((), ())), preferred_element_type=f32)


def dot_tn(left, right):
    return lax.dot_general(left, right, (((0,), (0,)), ((), ())), preferred_element_type=f32)


def mean(values):
    return jnp.sum(values, axis=1, keepdims=True) * (1.0 / values.shape[1])


def spans(length, block):
    return [(start, max(0, start - MOST), min(length, start + block + MOST)) for start in range(0, length, block)]


def make_marks(lengths, row, marks):
    length, count = marks.shape[1], lengths.shape[1]
    position = lax.broadcasted_iota(jnp.int32, (length, 128), 0)
    lane = lax.broadcasted_iota(jnp.int32, (length, 128), 1)
    number, end = jnp.zeros((length, 128), jnp.int32), jnp.int32(0)
    for pair in range(count):
        end = end + lengths[row, pair]
        number = number + (position >= end).astype(jnp.int32)
    for head in (0, 1):
        at = lane - HALF * (1 - head)
        used = (at >= 0) & (at < count)
        marks[head] = jnp.where(used & (number == at), 1.0, 0.0).astype(bf16)
        marks[2 + head] = jnp.where(used & (number != at), NEVER, 0.0).astype(bf16)


def lanes(head, value=1.0):
    lane = lax.broadcasted_iota(jnp.int32, (16, 128), 1)
    return jnp.where((lane < HALF) if head == 0 else (lane >= HALF), value, 0.0).astype(bf16)[:1]


def spread(half, width, share):
    source = lax.broadcasted_iota(jnp.int32, (half, width), 0)
    target = lax.broadcasted_iota(jnp.int32, (half, width), 1)
    return jnp.where(source % share == target % share, 1.0, 0.0).astype(bf16)


def load_weights(spot, blocks, weights, vector_blocks, sem):
    z, y, x, core = spot[0], spot[1], spot[2], spot[3]
    copies = []
    rows = 48
    half = weights.shape[2] // 2
    for index, block in enumerate(blocks):
        side = core if index < 4 else 1 - core
        columns = pl.ds(pl.multiple_of(side * half, 128), half)
        for near in (0, 1):
            for step in range(4):
                far = index % 2
                if index % 4 < 2:
                    cy, cx = jnp.bitwise_xor(y, far), jnp.bitwise_xor(x, near)
                else:
                    cy, cx = jnp.bitwise_xor(y, near), jnp.bitwise_xor(x, far)
                chip = lax.rem(z - step + 4, 4) * 4 + cy * 2 + cx
                target = pl.ds(pl.multiple_of(chip * rows, 16), rows)
                at = near * 4 + step
                for unit in (0, 1):
                    matrix = unit if index % 4 < 2 else 2 + unit
                    copies.append(
                        pltpu.make_async_copy(
                            block.at[at, pl.ds(unit * rows, rows)], weights.at[matrix, target, columns], sem
                        )
                    )
                if index % 4 >= 2:
                    copies.append(
                        pltpu.make_async_copy(
                            block.at[at, pl.ds(2 * rows, 16)], vector_blocks.at[chip * 2 + side], sem
                        )
                    )
    for copy in copies:
        copy.start()
    for copy in copies:
        copy.wait()


def spread_vectors(vector_blocks, vec, share):
    devices, _, half = vector_blocks.shape
    width = vec.shape[1]
    groups = 12
    entries = jnp.sum(vector_blocks[...].astype(f32), axis=1)
    lane = lax.broadcasted_iota(jnp.int32, (devices, half), 1)
    parts = [jnp.where(lane // share == group, entries, 0.0) for group in range(groups)]
    wide = dot(cat(parts).astype(bf16), spread(half, width, share))
    owner = lax.broadcasted_iota(jnp.int32, (devices, width), 1) // share
    device = lax.broadcasted_iota(jnp.int32, (devices, width), 0)
    for group in range(groups):
        part = wide[group * devices : (group + 1) * devices]
        vec[group : group + 1, :] = jnp.sum(jnp.where(owner == device, part, 0.0), axis=0, keepdims=True)


def attend_kernel(known, block, share, lengths, spot, x, *refs):
    if known:
        blocks, refs = refs[:8], refs[8:]
        q_out, k_out, v_out, mixed, lse, normed, inverse, w, vec, marks, vector_blocks, sem = refs
    else:
        w, vec, q_out, k_out, v_out, mixed, lse, normed, inverse, marks = refs
    row = pl.program_id(0)
    length, width = x.shape
    make_marks(lengths, row, marks)
    if known:

        @pl.when(row == 0)
        def _():
            load_weights(spot, blocks, w, vector_blocks, sem)
            spread_vectors(vector_blocks, vec, share)

    tokens = x[...]
    q_out[...] = (dot(tokens, w[0]) + vec[0:1, :]).astype(bf16)
    k_out[...] = dot(tokens, w[1]).astype(bf16)
    v_out[...] = (dot(tokens, w[2]) + vec[1:2, :]).astype(bf16)
    keep = (lanes(0), lanes(1))
    keep_scaled = (lanes(0, 0.125), lanes(1, 0.125))
    pairs, parts = width // 128, spans(length, block)

    def scores_of(pair):
        tile = pl.ds(pair * 128, 128)
        q, k, v = q_out[:, tile], k_out[:, tile], v_out[:, tile]
        qs = [q * keep_scaled[h] + marks[h] for h in (0, 1)]
        ks = [k * keep[h] + marks[2 + h] for h in (0, 1)]
        vs = [v * keep[h] + keep[1 - h] for h in (0, 1)]
        scores = [
            [dot_nt(ks[h][first:last], qs[h][start : start + block]) for h in (0, 1)] for start, first, last in parts
        ]
        return scores, vs

    upcoming = scores_of(0)
    for pair in range(pairs):
        scores, vs = upcoming
        if pair + 1 < pairs:
            upcoming = scores_of(pair + 1)
        tops = [[jnp.max(s, axis=0, keepdims=True) for s in both] for both in scores]
        probs = [[jnp.exp(s - t).astype(bf16) for s, t in zip(both, top)] for both, top in zip(scores, tops)]
        mixes = [
            [dot_tn(vs[h][first:last], probs[i][h]) for h in (0, 1)] for i, (start, first, last) in enumerate(parts)
        ]
        for i, (start, first, last) in enumerate(parts):
            out = []
            for h in (0, 1):
                mix = mixes[i][h]
                total = mix[HALF : HALF + 1] if h == 0 else mix[:1]
                lse[0, 2 * pair + h : 2 * pair + h + 1, start : start + block] = tops[i][h] + jnp.log(total)
                out.append((mix[:HALF] if h == 0 else mix[HALF:]) * (1.0 / total))
            mixed[start : start + block, pair * 128 : pair * 128 + 128] = jnp.transpose(cat(out)).astype(bf16)
    for start in range(0, length, 256):
        rows = pl.ds(start, 256)
        total = x[rows, :].astype(f32) + dot(mixed[rows, :], w[3]) + vec[2:3, :]
        centred = total - mean(total)
        inv = lax.rsqrt(mean(centred * centred) + EPSILON)
        normed[rows, :] = centred * inv
        inverse[rows, :] = jnp.broadcast_to(inv, (256, 128))


def attend_forward(known, x, gathered, lengths, spot, rows, share, block=128):
    tokens, width = x.shape
    length = tokens // rows
    shape = jax.ShapeDtypeStruct
    tile = pl.BlockSpec((length, width), lambda r, *_: (r, 0))
    fixed = [pl.BlockSpec((4, width, width), lambda r, *_: (0, 0, 0)), pl.BlockSpec((16, width), lambda r, *_: (0, 0))]
    act = shape((tokens, width), bf16)
    out_specs = [tile] * 4 + [
        pl.BlockSpec((1, 16, length), lambda r, *_: (r, 0, 0)),
        tile,
        pl.BlockSpec((length, 128), lambda r, *_: (r, 0)),
    ]
    out_shape = [act] * 4 + [shape((rows, 16, length), f32), shape((tokens, width), f32), shape((tokens, 128), f32)]
    scratch = [pltpu.VMEM((4, length, 128), bf16)]
    if known:
        in_specs = [tile] + [pl.BlockSpec(memory_space=pl.ANY)] * 8
        out_specs, out_shape = out_specs + fixed, out_shape + [shape((4, width, width), bf16), shape((16, width), f32)]
        scratch += [pltpu.VMEM((32, 16, width // 2), bf16), pltpu.SemaphoreType.DMA]
    else:
        in_specs = [tile] + fixed
    return pl.pallas_call(
        functools.partial(attend_kernel, known, block, share),
        grid_spec=pltpu.PrefetchScalarGridSpec(
            num_scalar_prefetch=2, grid=(rows,), in_specs=in_specs, out_specs=out_specs, scratch_shapes=scratch
        ),
        out_shape=out_shape,
        compiler_params=pltpu.CompilerParams(vmem_limit_bytes=60 * MEGA),
        cost_estimate=pl.CostEstimate(flops=10 * 10**9, bytes_accessed=2 * 10**7, transcendentals=4 * 10**6),
        name="attend",
    )(lengths, spot, x, *gathered)


def back_kernel(block, lengths, q_in, k_in, v_in, mixed, lse, grad, dq_out, dk_out, dv_out, marks):
    row = pl.program_id(0)
    length, width = q_in.shape
    make_marks(lengths, row, marks)
    keep = (lanes(0), lanes(1))
    keep_scaled = (lanes(0, 0.125), lanes(1, 0.125))
    head_of = lax.broadcasted_iota(jnp.int32, (16, 128), 1) // HALF
    picker = jnp.where(lax.broadcasted_iota(jnp.int32, (16, 128), 0) == head_of, 1.0, 0.0).astype(bf16)
    pairs, parts = width // 128, spans(length, block)

    def products_of(pair):
        tile = pl.ds(pair * 128, 128)
        q, k, v, g = q_in[:, tile], k_in[:, tile], v_in[:, tile], grad[:, tile]
        product = g.astype(f32) * mixed[:, tile].astype(f32)
        high = product.astype(bf16)
        centre = dot_nt(picker, high) + dot_nt(picker, (product - high.astype(f32)).astype(bf16))
        qz = [q * keep_scaled[h] for h in (0, 1)]
        kz = [k * keep[h] for h in (0, 1)]
        vz = [v * keep[h] for h in (0, 1)]
        gz = [g * keep[h] for h in (0, 1)]
        qs = [qz[h] + marks[h] for h in (0, 1)]
        ks = [kz[h] + marks[2 + h] for h in (0, 1)]
        scores = [
            [dot_nt(ks[h][start : start + block], qs[h][first:last]) for h in (0, 1)] for start, first, last in parts
        ]
        slopes = [
            [dot_nt(vz[h][start : start + block], g[first:last]) for h in (0, 1)] for start, first, last in parts
        ]
        return scores, slopes, centre, qz, kz, gz

    upcoming = products_of(0)
    for pair in range(pairs):
        scores, slopes, centre, qz, kz, gz = upcoming
        if pair + 1 < pairs:
            upcoming = products_of(pair + 1)
        probs, grads = [], []
        for i, (start, first, last) in enumerate(parts):
            prob = [jnp.exp(scores[i][h] - lse[0, 2 * pair + h : 2 * pair + h + 1, first:last]) for h in (0, 1)]
            probs.append([p.astype(bf16) for p in prob])
            grads.append([(prob[h] * (slopes[i][h] - centre[h : h + 1, first:last])).astype(bf16) for h in (0, 1)])
        columns = slice(pair * 128, pair * 128 + 128)
        to_values = [
            sum(dot(probs[i][h], gz[h][first:last]) for h in (0, 1)) for i, (start, first, last) in enumerate(parts)
        ]
        to_keys = [
            sum(dot(grads[i][h], qz[h][first:last]) for h in (0, 1)) for i, (start, first, last) in enumerate(parts)
        ]
        to_queries = [
            sum(dot_tn(grads[i][h], kz[h][start : start + block]) for h in (0, 1))
            for i, (start, first, last) in enumerate(parts)
        ]
        for i, (start, first, last) in enumerate(parts):
            dv_out[start : start + block, columns] = to_values[i].astype(bf16)
            dk_out[start : start + block, columns] = to_keys[i].astype(bf16)
        for at in range(0, length, MOST):
            pieces = [
                to_queries[i][at - first : at - first + MOST]
                for i, (start, first, last) in enumerate(parts)
                if first <= at < last
            ]
            dq_out[at : at + MOST, columns] = (sum(pieces) * 0.125).astype(bf16)


def attend_back(q, k, v, mixed, lse, grad, lengths, rows, block=128):
    tokens, width = q.shape
    length = tokens // rows
    tile = pl.BlockSpec((length, width), lambda r, *_: (r, 0))
    return pl.pallas_call(
        functools.partial(back_kernel, block),
        grid_spec=pltpu.PrefetchScalarGridSpec(
            num_scalar_prefetch=1,
            grid=(rows,),
            in_specs=[tile] * 4 + [pl.BlockSpec((1, 16, length), lambda r, *_: (r, 0, 0)), tile],
            out_specs=[tile] * 3,
            scratch_shapes=[pltpu.VMEM((4, length, 128), bf16)],
        ),
        out_shape=[jax.ShapeDtypeStruct((tokens, width), bf16)] * 3,
        compiler_params=pltpu.CompilerParams(vmem_limit_bytes=60 * MEGA),
        cost_estimate=pl.CostEstimate(flops=12 * 10**9, bytes_accessed=2 * 10**7, transcendentals=4 * 10**6),
        name="attend_back",
    )(lengths, q, k, v, mixed, lse, grad)


def gelu_parts(u):
    bell = jnp.exp(u * u * -0.5)
    t = 1.0 / (1.0 + (0.3275911 * SQRT_HALF) * jnp.abs(u))
    poly = t * (0.127414796 + t * (-0.142248368 + t * (0.7107068705 + t * (-0.7265760135 + t * 0.5307027145))))
    tail = poly * bell
    phi = jnp.where(u >= 0.0, 1.0 - tail, tail)
    return u * phi, phi + u * (bell * INV_ROOT)


def ffn_kernel(
    chunks, size, weights, normed, inverse, cot, mixed, out_mat, vec, layer_out, grads, first, grad_mixed, grad_out, sums,
    w, low, act, slope, total, second_low, back, ready, loaded, sent,
):
    tokens, width = normed.shape
    copies = []
    for i in range(2 * chunks):
        columns = pl.ds(i * width, width)
        copies.append(pltpu.make_async_copy(weights.at[:, columns], w.at[:, columns], loaded.at[i]))
        copies[i].start()
    gain, shift = vec[3:4, :], vec[4:5, :]
    down_add, final_gain, final_shift = vec[5:6, :], vec[6:7, :], vec[7:8, :]

    def up(g):
        return w[:, g * width : (g + 1) * width]

    def down(g):
        return w[:, (chunks + g) * width : (chunks + g + 1) * width]

    low[...] = (normed[...] * gain + shift).astype(bf16)
    sums[...] = jnp.zeros_like(sums)
    for copy in copies:
        copy.wait()

    def forward(t, _):
        rows = pl.ds(pl.multiple_of(t * size, size), size)
        inputs = low[rows, :]
        pre, added = dot(inputs, up(0)), None
        for g in range(chunks):
            upcoming = dot(inputs, up(g + 1)) if g + 1 < chunks else None
            activated, derivative = gelu_parts(pre + vec[8 + g : 9 + g, :])
            activated = activated.astype(bf16)
            act[g, rows, :] = activated
            slope[g, rows, :] = derivative.astype(bf16)
            part = dot(activated, down(g))
            added = part if added is None else added + part
            pre = upcoming
        second_sum = normed[rows, :] * gain + shift + added + down_add
        centred = second_sum - mean(second_sum)
        inv = lax.rsqrt(mean(centred * centred) + EPSILON)
        hat = centred * inv
        layer_out[rows, :] = (hat * final_gain + final_shift).astype(bf16)
        grad = cot[rows, :].astype(f32)
        scaled = grad * final_gain
        second = inv * (scaled - mean(scaled) - hat * mean(scaled * hat))
        total[rows, :] = second
        second_low[rows, :] = second.astype(bf16)
        sums[0:1, :] += jnp.sum(second, axis=0, keepdims=True)
        sums[1:2, :] += jnp.sum(grad * hat, axis=0, keepdims=True)
        sums[2:3, :] += jnp.sum(grad, axis=0, keepdims=True)
        return 0

    lax.fori_loop(0, tokens // size, forward, 0)
    pending = []
    for g in range(chunks):
        to_act = dot_nt(second_low[...], down(g))
        to_down = dot_tn(act[g], second_low[...])
        to_pre = to_act * slope[g].astype(f32)
        sums[6 + g : 7 + g, :] = jnp.sum(to_pre, axis=0, keepdims=True)
        back[...] = to_pre.astype(bf16)
        slot = g % 2
        if g >= 2:
            for copy in pending[g - 2]:
                copy.wait()
        ready[slot, 1] = to_down.astype(bf16)
        total[...] += dot_nt(back[...], up(g))
        ready[slot, 0] = dot_tn(low[...], back[...]).astype(bf16)
        out = [
            pltpu.make_async_copy(
                ready.at[slot, j], grads.at[:, pl.ds((j * chunks + g) * width, width)], sent.at[slot, j]
            )
            for j in (0, 1)
        ]
        for copy in out:
            copy.start()
        pending.append(out)

    def backward(t, _):
        rows = pl.ds(pl.multiple_of(t * size, size), size)
        middle, hat, inv = total[rows, :], normed[rows, :], inverse[rows, 0:1]
        scaled = middle * gain
        to_first = inv * (scaled - mean(scaled) - hat * mean(scaled * hat))
        first[rows, :] = to_first
        to_low = to_first.astype(bf16)
        second_low[rows, :] = to_low
        sums[3:4, :] += jnp.sum(middle * hat, axis=0, keepdims=True)
        sums[4:5, :] += jnp.sum(middle, axis=0, keepdims=True)
        sums[5:6, :] += jnp.sum(to_first, axis=0, keepdims=True)
        grad_mixed[rows, :] = dot_nt(to_low, out_mat[0]).astype(bf16)
        return 0

    lax.fori_loop(0, tokens // size, backward, 0)
    grad_out[...] = dot_tn(mixed[...], second_low[...]).astype(bf16)
    for out in pending[-2:]:
        for copy in out:
            copy.wait()


def ffn(weights, normed, inverse, cot, mixed, mats, vec, size=256):
    tokens, width = normed.shape
    chunks = weights.shape[1] // (2 * width)
    shape = jax.ShapeDtypeStruct

    def full(value):
        return pl.BlockSpec(value.shape, lambda i: (0,) * len(value.shape))

    outs = [
        shape((tokens, width), bf16),
        shape(weights.shape, bf16),
        shape((tokens, width), f32),
        shape((tokens, width), bf16),
        shape((width, width), bf16),
        shape((16, width), f32),
    ]
    out_specs = [full(out) for out in outs]
    out_specs[1] = pl.BlockSpec(memory_space=pl.ANY)
    return pl.pallas_call(
        functools.partial(ffn_kernel, chunks, size),
        grid=(1,),
        in_specs=[
            pl.BlockSpec(memory_space=pl.ANY),
            full(normed),
            full(inverse),
            full(cot),
            full(mixed),
            pl.BlockSpec((1, width, width), lambda i: (3, 0, 0)),
            full(vec),
        ],
        out_specs=out_specs,
        out_shape=outs,
        scratch_shapes=[
            pltpu.VMEM(weights.shape, bf16),
            pltpu.VMEM((tokens, width), bf16),
            pltpu.VMEM((chunks, tokens, width), bf16),
            pltpu.VMEM((chunks, tokens, width), bf16),
            pltpu.VMEM((tokens, width), f32),
            pltpu.VMEM((tokens, width), bf16),
            pltpu.VMEM((tokens, width), bf16),
            pltpu.VMEM((2, 2, width, width), bf16),
            pltpu.SemaphoreType.DMA((2 * chunks,)),
            pltpu.SemaphoreType.DMA((2, 2)),
        ],
        compiler_params=pltpu.CompilerParams(vmem_limit_bytes=63 * MEGA),
        cost_estimate=pl.CostEstimate(flops=32 * 10**9, bytes_accessed=3 * 10**7, transcendentals=6 * 10**6),
        name="ffn",
    )(weights, normed, inverse, cot, mixed, mats, vec)


def weight_kernel(share, spot, x, dq, dk, dv, grad_out, sums, keep, away):
    core = spot[3]
    tokens, width = x.shape
    half, chips, rows = width // 2, keep.shape[0], 2 * share
    natural = [jnp.sum(dq[...].astype(f32), axis=0, keepdims=True), jnp.sum(dv[...].astype(f32), axis=0, keepdims=True)]
    natural += [sums[i : i + 1, :] for i in (5, 3, 4, 0, 1, 2, 6, 7, 8, 9)]
    owner = lax.broadcasted_iota(jnp.int32, (chips, width), 1) // share
    chip = lax.broadcasted_iota(jnp.int32, (chips, width), 0)
    lane = lax.broadcasted_iota(jnp.int32, (chips, half), 1)
    table = spread(half, width, share)
    top = lax.broadcasted_iota(jnp.int32, (chips, 16, half), 1) == 0
    for side, out in ((1 - core, away), (core, keep)):
        columns = pl.ds(pl.multiple_of(side * half, 128), half)
        for unit, grad in enumerate((dq, dk, dv)):
            block = dot_tn(x[...], grad[:, columns]).astype(bf16)
            out[:, unit * rows : (unit + 1) * rows, :] = block.reshape(chips, rows, half)
        out[:, 3 * rows : 4 * rows, :] = grad_out[:, columns].reshape(chips, rows, half)
        mine = owner == 2 * chip + side
        entries = jnp.zeros((chips, half), f32)
        spreads = dot_nt(cat([jnp.where(mine, row, 0.0) for row in natural]).astype(bf16), table)
        for group in range(len(natural)):
            part = spreads[group * chips : (group + 1) * chips]
            entries = entries + jnp.where(lane // share == group, part, 0.0)
        out[:, 4 * rows :, :] = jnp.where(top, entries[:, None, :], 0.0).astype(bf16)


def weight_blocks(x, dq, dk, dv, grad_out, sums, spot, share):
    width = x.shape[1]
    blocks = jax.ShapeDtypeStruct((16, 8 * share + 16, width // 2), bf16)
    vmem = pl.BlockSpec(memory_space=pltpu.VMEM)
    return pl.pallas_call(
        functools.partial(weight_kernel, share),
        in_specs=[pl.BlockSpec(memory_space=pltpu.SMEM)] + [vmem] * 6,
        out_specs=[vmem] * 2,
        out_shape=[blocks] * 2,
        compiler_params=pltpu.CompilerParams(vmem_limit_bytes=60 * MEGA),
        cost_estimate=pl.CostEstimate(flops=4 * 10**9, bytes_accessed=10**7, transcendentals=0),
        name="weight_blocks",
    )(spot, x, dq, dk, dv, grad_out, sums)


def outer_sum(left, right):
    return jnp.einsum("ta,tb->ab", left, right, preferred_element_type=jnp.float32)


def back_product(grads, weights):
    return jnp.einsum("tb,ab->ta", grads, weights, preferred_element_type=jnp.float32)


def per_device(
    known,
    hidden,
    pair_lengths,
    cotangent,
    query_weight,
    query_bias,
    key_weight,
    value_weight,
    value_bias,
    out_weight,
    out_bias,
    attn_gain,
    attn_shift,
    up_weight,
    up_bias,
    down_weight,
    down_bias,
    final_gain,
    final_shift,
):
    rows_here, length, width = hidden.shape
    count = rows_here * length
    share = query_weight.shape[0]
    devices = width // share
    chunks = up_weight.shape[1] // width
    up_mine = (
        up_weight.reshape(share, devices, chunks, share).swapaxes(1, 2).reshape(share, chunks * width)
    )
    down_mine = down_weight.reshape(chunks, share, width).swapaxes(0, 1).reshape(share, chunks * width)
    ffn_mine = cat([up_mine, down_mine], 1)
    ffn_full = lax.all_gather(ffn_mine, AXES, axis=0, tiled=True)
    vector = cat(
        [
            query_bias,
            value_bias,
            out_bias,
            attn_gain,
            attn_shift,
            down_bias,
            final_gain,
            final_shift,
            up_bias,
        ]
    )
    matrices = jnp.stack([query_weight, key_weight, value_weight, out_weight])
    tokens = hidden.reshape(count, width)
    groups = 8 + chunks
    z, y, x, core = place()
    if known:
        spot = jnp.stack([z, y, x, core]).astype(jnp.int32)
        gathered = gather_attention(matrices, vector)
        out = attend_forward(True, tokens, gathered, pair_lengths, spot, rows_here, share)
        queries, keys_all, values_all, mixed, log_totals, first_norm, first_inverse, mats, vec = out
    else:
        spot = jnp.zeros((4,), jnp.int32)
        mats, vectors = gather_attention_any(matrices, vector)
        vec = vectors.reshape(devices, groups, share).swapaxes(0, 1).reshape(groups, width).astype(f32)
        vec = jnp.pad(vec, ((0, 16 - groups), (0, 0)))
        out = attend_forward(False, tokens, (mats, vec), pair_lengths, spot, rows_here, share)
        queries, keys_all, values_all, mixed, log_totals, first_norm, first_inverse = out
    layer_out, ffn_grads, grad_first, grad_mixed, grad_out_weight, sums = ffn(
        ffn_full, first_norm, first_inverse, cotangent.reshape(count, width), mixed, mats, vec
    )
    ffn_owned = lax.psum_scatter(ffn_grads, AXES, scatter_dimension=0, tiled=True).astype(f32)
    grad_queries, grad_keys, grad_values = attend_back(
        queries, keys_all, values_all, mixed, log_totals, grad_mixed, pair_lengths, rows_here
    )
    if known:
        keep, away = weight_blocks(tokens, grad_queries, grad_keys, grad_values, grad_out_weight, sums, spot, share)
        mats_owned, vectors_owned = scatter_attention(keep, away, 4, share, groups * share)
    else:
        mat_grads = jnp.stack(
            [
                outer_sum(tokens, grad_queries),
                outer_sum(tokens, grad_keys),
                outer_sum(tokens, grad_values),
                grad_out_weight.astype(f32),
            ]
        )
        biases = jnp.stack([jnp.sum(grad_queries.astype(f32), 0), jnp.sum(grad_values.astype(f32), 0)])
        vector_grads = cat([biases, sums[5:6], sums[3:5], sums[:3], sums[6 : 6 + chunks]])
        vector_grads = vector_grads.reshape(groups, devices, share).swapaxes(0, 1).reshape(devices, groups * share)
        mats_owned, vectors_owned = scatter_attention_any(mat_grads, vector_grads)
    grad_tokens = (
        grad_first
        + back_product(grad_queries, mats[0])
        + back_product(grad_keys, mats[1])
        + back_product(grad_values, mats[2])
    )
    own = vectors_owned.reshape(8 + chunks, share)
    up_owned = (
        ffn_owned[:, : chunks * width]
        .reshape(share, chunks, devices, share)
        .swapaxes(1, 2)
        .reshape(share, chunks * width)
    )
    down_owned = (
        ffn_owned[:, chunks * width :].reshape(share, chunks, width).swapaxes(0, 1).reshape(chunks * share, width)
    )
    return (
        layer_out.reshape(hidden.shape),
        grad_tokens.reshape(hidden.shape),
        mats_owned[0],
        own[0],
        mats_owned[1],
        mats_owned[2],
        own[1],
        mats_owned[3],
        own[2],
        own[3],
        own[4],
        up_owned,
        own[8:].reshape(chunks * share),
        down_owned,
        own[5],
        own[6],
        own[7],
    )


def solution(mesh):
    known = dict(mesh.shape) == {"dp": 8, "shard": 4}
    cube, flat, line = P(AXES, None, None), P(AXES, None), P(AXES)
    return jax.shard_map(
        lambda *args: per_device(known, *args),
        mesh=mesh,
        in_specs=(
            cube, flat, cube, flat, line, flat, flat, line, flat, line, line, line, flat, line, flat, line, line, line,
        ),
        out_specs=(
            cube, cube, flat, line, flat, flat, line, flat, line, line, line, flat, line, flat, line, line, line,
        ),
        check_vma=False,
    )
```

```python
import functools

import jax
import jax.numpy as jnp
from jax import lax
from jax.experimental import pallas as pl
from jax.experimental.pallas import tpu as pltpu
from jax.sharding import Mesh
from jax.sharding import PartitionSpec as P

EPSILON = 1e-06
SQRT_HALF = 0.7071067811865476
INV_ROOT = 0.3989422804014327
MOST = 128
HALF = 64
NEVER = -1e30
MEGA = 1024 * 1024

AXES = ("dp", "shard")
CHIPS = ("z", "y", "x", "core")
f32 = jnp.float32
bf16 = jnp.bfloat16
cat = jnp.concatenate


def moves(move):
    pairs = []
    for index in range(32):
        z, y, x, core = index // 8, (index // 4) % 2, (index // 2) % 2, index % 2
        z, y, x, core = move(z, y, x, core)
        pairs.append((index, z * 8 + y * 4 + x * 2 + core))
    return pairs


MOVES = {
    "core": moves(lambda z, y, x, core: (z, y, x, 1 - core)),
    "x": moves(lambda z, y, x, core: (z, y, 1 - x, core)),
    "y": moves(lambda z, y, x, core: (z, 1 - y, x, core)),
    "z1": moves(lambda z, y, x, core: ((z + 1) % 4, y, x, core)),
    "z2": moves(lambda z, y, x, core: ((z + 2) % 4, y, x, core)),
    "z3": moves(lambda z, y, x, core: ((z + 3) % 4, y, x, core)),
}


def send(values, move):
    return lax.ppermute(values, CHIPS, MOVES[move])


def place():
    return tuple(lax.axis_index(axis) for axis in CHIPS)


def phase(*values):
    return lax.optimization_barrier(values)


def add(*terms):
    total = terms[0].astype(f32)
    for term in terms[1:]:
        total = total + term.astype(f32)
    return total


def gather_blocks(block, split):
    one, two, three = send(block, "z1"), send(block, "z2"), send(block, "z3")
    one, two, three = phase(one, two, three)
    line = jnp.stack([block, one, two, three])
    first, second = line[:, :split], line[:, split:]
    first_x, second_y = send(first, "x"), send(second, "y")
    first_x, second_y, first, second = phase(first_x, second_y, first, second)
    first, second = cat([first, first_x]), cat([second, second_y])
    first_y, second_x = send(first, "y"), send(second, "x")
    other_first, other_second = send(first, "core"), send(second, "core")
    first, first_y, second, second_x, other_first, other_second = phase(
        first, first_y, second, second_x, other_first, other_second
    )
    other_first_y, other_second_x = send(first_y, "core"), send(second_x, "core")
    return first, first_y, second, second_x, other_first, other_first_y, other_second, other_second_x


def pick(values, index, axis):
    return lax.dynamic_index_in_dim(values, index, axis, False)


def send_line(parts):
    return tuple(send(part, move) for part, move in zip(parts, ("z1", "z2", "z3")))


def halves_of(mine):
    z, y, x, core = place()
    kept = pick(mine, core, 1)
    got = send(pick(mine, 1 - core, 1).astype(bf16), "core").astype(f32)
    return jnp.where(core == 0, cat([kept, got], 2), cat([got, kept], 2))


def gather_attention(matrices, vector):
    z, y, x, core = place()
    count, rows, width = matrices.shape
    half = width // 2
    mine = lax.dynamic_slice_in_dim(matrices, core * half, half, 2)
    got = send(lax.dynamic_slice_in_dim(matrices, (1 - core) * half, half, 2), "core")
    pair = jnp.where(core == 0, cat([mine, got], 1), cat([got, mine], 1))
    vector_rows = jnp.pad(vector[None], ((0, 15), (0, half - vector.shape[0])))
    block = cat([pair.reshape(count * 2 * rows, half), vector_rows])
    (block,) = phase(block)
    return gather_blocks(block, count * rows)


def gather_attention_any(matrices, vector):
    mats = lax.all_gather(matrices, AXES, axis=1, tiled=True)
    return mats, lax.all_gather(vector, AXES, axis=0, tiled=False)


def scatter_attention_any(matrices, vectors):
    mats = lax.psum_scatter(matrices.astype(bf16), AXES, scatter_dimension=1, tiled=True)
    return mats.astype(f32), lax.psum_scatter(vectors, AXES, scatter_dimension=0, tiled=False)


def dot(left, right):
    return lax.dot_general(left, right, (((1,), (0,)), ((), ())), preferred_element_type=f32)


def dot_nt(left, right):
    return lax.dot_general(left, right, (((1,), (1,)), ((), ())), preferred_element_type=f32)


def dot_tn(left, right):
    return lax.dot_general(left, right, (((0,), (0,)), ((), ())), preferred_element_type=f32)


def mean(values):
    return jnp.sum(values, axis=1, keepdims=True) * (1.0 / values.shape[1])


def spans(length, block):
    return [(start, max(0, start - MOST), min(length, start + block + MOST)) for start in range(0, length, block)]


def make_marks(lengths, row, marks):
    length, count = marks.shape[1], lengths.shape[1]
    position = lax.broadcasted_iota(jnp.int32, (length, 128), 0)
    lane = lax.broadcasted_iota(jnp.int32, (length, 128), 1)
    number, end = jnp.zeros((length, 128), jnp.int32), jnp.int32(0)
    for pair in range(count):
        end = end + lengths[row, pair]
        number = number + (position >= end).astype(jnp.int32)
    for head in (0, 1):
        at = lane - HALF * (1 - head)
        used = (at >= 0) & (at < count)
        marks[head] = jnp.where(used & (number == at), 1.0, 0.0).astype(bf16)
        marks[2 + head] = jnp.where(used & (number != at), NEVER, 0.0).astype(bf16)


def lanes(head, value=1.0):
    lane = lax.broadcasted_iota(jnp.int32, (16, 128), 1)
    return jnp.where((lane < HALF) if head == 0 else (lane >= HALF), value, 0.0).astype(bf16)[:1]


def spread(half, width, share):
    source = lax.broadcasted_iota(jnp.int32, (half, width), 0)
    target = lax.broadcasted_iota(jnp.int32, (half, width), 1)
    return jnp.where(source % share == target % share, 1.0, 0.0).astype(bf16)


def load_weights(spot, blocks, weights, vector_blocks, sem):
    z, y, x, core = spot[0], spot[1], spot[2], spot[3]
    copies = []
    rows = 48
    half = weights.shape[2] // 2
    for index, block in enumerate(blocks):
        side = core if index < 4 else 1 - core
        columns = pl.ds(pl.multiple_of(side * half, 128), half)
        for near in (0, 1):
            for step in range(4):
                far = index % 2
                if index % 4 < 2:
                    cy, cx = jnp.bitwise_xor(y, far), jnp.bitwise_xor(x, near)
                else:
                    cy, cx = jnp.bitwise_xor(y, near), jnp.bitwise_xor(x, far)
                chip = lax.rem(z - step + 4, 4) * 4 + cy * 2 + cx
                target = pl.ds(pl.multiple_of(chip * rows, 16), rows)
                at = near * 4 + step
                for unit in (0, 1):
                    matrix = unit if index % 4 < 2 else 2 + unit
                    copies.append(
                        pltpu.make_async_copy(
                            block.at[at, pl.ds(unit * rows, rows)], weights.at[matrix, target, columns], sem
                        )
                    )
                if index % 4 >= 2:
                    copies.append(
                        pltpu.make_async_copy(
                            block.at[at, pl.ds(2 * rows, 16)], vector_blocks.at[chip * 2 + side], sem
                        )
                    )
    for copy in copies:
        copy.start()
    for copy in copies:
        copy.wait()


def spread_vectors(vector_blocks, vec, share):
    devices, _, half = vector_blocks.shape
    width = vec.shape[1]
    groups = 12
    entries = jnp.sum(vector_blocks[...].astype(f32), axis=1)
    lane = lax.broadcasted_iota(jnp.int32, (devices, half), 1)
    parts = [jnp.where(lane // share == group, entries, 0.0) for group in range(groups)]
    wide = dot(cat(parts).astype(bf16), spread(half, width, share))
    owner = lax.broadcasted_iota(jnp.int32, (devices, width), 1) // share
    device = lax.broadcasted_iota(jnp.int32, (devices, width), 0)
    for group in range(groups):
        part = wide[group * devices : (group + 1) * devices]
        vec[group : group + 1, :] = jnp.sum(jnp.where(owner == device, part, 0.0), axis=0, keepdims=True)


def attend_kernel(known, block, share, lengths, spot, x, *refs):
    if known:
        blocks, refs = refs[:8], refs[8:]
        q_out, k_out, v_out, mixed, lse, normed, inverse, w, vec, marks, vector_blocks, sem = refs
    else:
        w, vec, q_out, k_out, v_out, mixed, lse, normed, inverse, marks = refs
    row = pl.program_id(0)
    length, width = x.shape
    make_marks(lengths, row, marks)
    if known:

        @pl.when(row == 0)
        def _():
            load_weights(spot, blocks, w, vector_blocks, sem)
            spread_vectors(vector_blocks, vec, share)

    tokens = x[...]
    q_out[...] = (dot(tokens, w[0]) + vec[0:1, :]).astype(bf16)
    k_out[...] = dot(tokens, w[1]).astype(bf16)
    v_out[...] = (dot(tokens, w[2]) + vec[1:2, :]).astype(bf16)
    keep = (lanes(0), lanes(1))
    keep_scaled = (lanes(0, 0.125), lanes(1, 0.125))
    pairs, parts = width // 128, spans(length, block)

    def scores_of(pair):
        tile = pl.ds(pair * 128, 128)
        q, k, v = q_out[:, tile], k_out[:, tile], v_out[:, tile]
        qs = [q * keep_scaled[h] + marks[h] for h in (0, 1)]
        ks = [k * keep[h] + marks[2 + h] for h in (0, 1)]
        vs = [v * keep[h] + keep[1 - h] for h in (0, 1)]
        scores = [
            [dot_nt(ks[h][first:last], qs[h][start : start + block]) for h in (0, 1)] for start, first, last in parts
        ]
        return scores, vs

    upcoming = scores_of(0)
    for pair in range(pairs):
        scores, vs = upcoming
        if pair + 1 < pairs:
            upcoming = scores_of(pair + 1)
        tops = [[jnp.max(s, axis=0, keepdims=True) for s in both] for both in scores]
        probs = [[jnp.exp(s - t).astype(bf16) for s, t in zip(both, top)] for both, top in zip(scores, tops)]
        mixes = [
            [dot_tn(vs[h][first:last], probs[i][h]) for h in (0, 1)] for i, (start, first, last) in enumerate(parts)
        ]
        for i, (start, first, last) in enumerate(parts):
            out = []
            for h in (0, 1):
                mix = mixes[i][h]
                total = mix[HALF : HALF + 1] if h == 0 else mix[:1]
                lse[0, 2 * pair + h : 2 * pair + h + 1, start : start + block] = tops[i][h] + jnp.log(total)
                out.append((mix[:HALF] if h == 0 else mix[HALF:]) * (1.0 / total))
            mixed[start : start + block, pair * 128 : pair * 128 + 128] = jnp.transpose(cat(out)).astype(bf16)
    for start in range(0, length, 256):
        rows = pl.ds(start, 256)
        total = x[rows, :].astype(f32) + dot(mixed[rows, :], w[3]) + vec[2:3, :]
        centred = total - mean(total)
        inv = lax.rsqrt(mean(centred * centred) + EPSILON)
        normed[rows, :] = centred * inv
        inverse[rows, :] = jnp.broadcast_to(inv, (256, 128))


def attend_forward(known, x, gathered, lengths, spot, rows, share, block=128):
    tokens, width = x.shape
    length = tokens // rows
    shape = jax.ShapeDtypeStruct
    tile = pl.BlockSpec((length, width), lambda r, *_: (r, 0))
    fixed = [pl.BlockSpec((4, width, width), lambda r, *_: (0, 0, 0)), pl.BlockSpec((16, width), lambda r, *_: (0, 0))]
    act = shape((tokens, width), bf16)
    out_specs = [tile] * 4 + [
        pl.BlockSpec((1, 16, length), lambda r, *_: (r, 0, 0)),
        tile,
        pl.BlockSpec((length, 128), lambda r, *_: (r, 0)),
    ]
    out_shape = [act] * 4 + [shape((rows, 16, length), f32), shape((tokens, width), f32), shape((tokens, 128), f32)]
    scratch = [pltpu.VMEM((4, length, 128), bf16)]
    if known:
        in_specs = [tile] + [pl.BlockSpec(memory_space=pl.ANY)] * 8
        out_specs, out_shape = out_specs + fixed, out_shape + [shape((4, width, width), bf16), shape((16, width), f32)]
        scratch += [pltpu.VMEM((32, 16, width // 2), bf16), pltpu.SemaphoreType.DMA]
    else:
        in_specs = [tile] + fixed
    return pl.pallas_call(
        functools.partial(attend_kernel, known, block, share),
        grid_spec=pltpu.PrefetchScalarGridSpec(
            num_scalar_prefetch=2, grid=(rows,), in_specs=in_specs, out_specs=out_specs, scratch_shapes=scratch
        ),
        out_shape=out_shape,
        compiler_params=pltpu.CompilerParams(vmem_limit_bytes=60 * MEGA),
        cost_estimate=pl.CostEstimate(flops=10 * 10**9, bytes_accessed=2 * 10**7, transcendentals=4 * 10**6),
        name="attend",
    )(lengths, spot, x, *gathered)


def natural_rows(bias_rows, first_sums, second_sums):
    rows = bias_rows + [second_sums[2:3, :], second_sums[0:1, :], second_sums[1:2, :]]
    rows += [first_sums[i : i + 1, :] for i in (0, 1, 2)]
    return rows + [first_sums[i : i + 1, :] for i in (3, 4, 5, 6)]


def back_kernel(known, block, share, lengths, spot, x, q_in, k_in, v_in, mixed, lse, grad, *refs):
    grad_out, first_sums, second_sums, dq_out, dk_out, dv_out, keep, away, marks = refs
    tokens, width = q_in.shape
    rows = lengths.shape[0]
    length = tokens // rows
    for row in range(rows):
        make_marks(lengths, row, marks.at[row])
    keep_lanes = (lanes(0), lanes(1))
    keep_scaled = (lanes(0, 0.125), lanes(1, 0.125))
    head_of = lax.broadcasted_iota(jnp.int32, (16, 128), 1) // HALF
    picker = jnp.where(lax.broadcasted_iota(jnp.int32, (16, 128), 0) == head_of, 1.0, 0.0).astype(bf16)
    parts = spans(length, block)
    items = [(row, pair) for row in range(rows) for pair in range(width // 128)]

    def products_of(row, pair):
        tile = (slice(row * length, row * length + length), slice(pair * 128, pair * 128 + 128))
        q, k, v, g = q_in[tile], k_in[tile], v_in[tile], grad[tile]
        product = g.astype(f32) * mixed[tile].astype(f32)
        high = product.astype(bf16)
        centre = dot_nt(picker, high) + dot_nt(picker, (product - high.astype(f32)).astype(bf16))
        qz = [q * keep_scaled[h] for h in (0, 1)]
        kz = [k * keep_lanes[h] for h in (0, 1)]
        vz = [v * keep_lanes[h] for h in (0, 1)]
        gz = [g * keep_lanes[h] for h in (0, 1)]
        qs = [qz[h] + marks[row, h] for h in (0, 1)]
        ks = [kz[h] + marks[row, 2 + h] for h in (0, 1)]
        scores = [
            [dot_nt(ks[h][start : start + block], qs[h][first:last]) for h in (0, 1)] for start, first, last in parts
        ]
        slopes = [
            [dot_nt(vz[h][start : start + block], g[first:last]) for h in (0, 1)] for start, first, last in parts
        ]
        return scores, slopes, centre, qz, kz, gz

    upcoming = products_of(*items[0])
    for index, (row, pair) in enumerate(items):
        scores, slopes, centre, qz, kz, gz = upcoming
        if index + 1 < len(items):
            upcoming = products_of(*items[index + 1])
        probs, grads = [], []
        for i, (start, first, last) in enumerate(parts):
            head = 2 * pair
            prob = [jnp.exp(scores[i][h] - lse[row, head + h : head + h + 1, first:last]) for h in (0, 1)]
            probs.append([p.astype(bf16) for p in prob])
            grads.append([(prob[h] * (slopes[i][h] - centre[h : h + 1, first:last])).astype(bf16) for h in (0, 1)])
        columns = slice(pair * 128, pair * 128 + 128)
        to_values = [
            sum(dot(probs[i][h], gz[h][first:last]) for h in (0, 1)) for i, (start, first, last) in enumerate(parts)
        ]
        to_keys = [
            sum(dot(grads[i][h], qz[h][first:last]) for h in (0, 1)) for i, (start, first, last) in enumerate(parts)
        ]
        to_queries = [
            sum(dot_tn(grads[i][h], kz[h][start : start + block]) for h in (0, 1))
            for i, (start, first, last) in enumerate(parts)
        ]
        base = row * length
        for i, (start, first, last) in enumerate(parts):
            dv_out[base + start : base + start + block, columns] = to_values[i].astype(bf16)
            dk_out[base + start : base + start + block, columns] = to_keys[i].astype(bf16)
        for at in range(0, length, MOST):
            pieces = [
                to_queries[i][at - first : at - first + MOST]
                for i, (start, first, last) in enumerate(parts)
                if first <= at < last
            ]
            dq_out[base + at : base + at + MOST, columns] = (sum(pieces) * 0.125).astype(bf16)
    biases = [jnp.sum(out[...].astype(f32), axis=0, keepdims=True) for out in (dq_out, dv_out)]
    if not known:
        for unit, out in enumerate((dq_out, dk_out, dv_out)):
            keep[unit] = dot_tn(x[...], out[...]).astype(bf16)
        away[...] = jnp.zeros_like(away)
        away[0:1, :] = biases[0]
        away[1:2, :] = biases[1]
        return
    core = spot[3]
    half, chips, size = width // 2, keep.shape[0], 2 * share
    natural = natural_rows(biases, first_sums, second_sums)
    owner = lax.broadcasted_iota(jnp.int32, (chips, width), 1) // share
    chip = lax.broadcasted_iota(jnp.int32, (chips, width), 0)
    lane = lax.broadcasted_iota(jnp.int32, (chips, half), 1)
    table = spread(half, width, share)
    top = lax.broadcasted_iota(jnp.int32, (chips, 16, half), 1) == 0
    for side, out in ((1 - core, away), (core, keep)):
        own = pl.ds(pl.multiple_of(side * half, 128), half)
        for unit, out_ref in enumerate((dq_out, dk_out, dv_out)):
            part = dot_tn(x[...], out_ref[:, own]).astype(bf16)
            out[:, unit * size : (unit + 1) * size, :] = part.reshape(chips, size, half)
        out[:, 3 * size : 4 * size, :] = grad_out[:, own].reshape(chips, size, half)
        mine = owner == 2 * chip + side
        entries = jnp.zeros((chips, half), f32)
        spreads = dot_nt(cat([jnp.where(mine, row, 0.0) for row in natural]).astype(bf16), table)
        for group in range(len(natural)):
            part = spreads[group * chips : (group + 1) * chips]
            entries = entries + jnp.where(lane // share == group, part, 0.0)
        out[:, 4 * size :, :] = jnp.where(top, entries[:, None, :], 0.0).astype(bf16)


def full_block(value):
    return pl.BlockSpec(value.shape, lambda i, *_: (0,) * len(value.shape))


def attend_back(known, share, spot, x, q, k, v, mixed, lse, grad, grad_out, first_sums, second_sums, lengths, block=128):
    tokens, width = q.shape
    rows = lengths.shape[0]
    shape = jax.ShapeDtypeStruct
    outs = [shape((tokens, width), bf16)] * 3
    if known:
        outs += [shape((16, 8 * share + 16, width // 2), bf16)] * 2
    else:
        outs += [shape((3, width, width), bf16), shape((8, width), f32)]
    inputs = (x, q, k, v, mixed, lse, grad, grad_out, first_sums, second_sums)
    return pl.pallas_call(
        functools.partial(back_kernel, known, block, share),
        grid_spec=pltpu.PrefetchScalarGridSpec(
            num_scalar_prefetch=2,
            grid=(1,),
            in_specs=[full_block(value) for value in inputs],
            out_specs=[full_block(out) for out in outs],
            scratch_shapes=[pltpu.VMEM((rows, 4, tokens // rows, 128), bf16)],
        ),
        out_shape=outs,
        compiler_params=pltpu.CompilerParams(vmem_limit_bytes=60 * MEGA),
        cost_estimate=pl.CostEstimate(flops=20 * 10**9, bytes_accessed=2 * 10**7, transcendentals=4 * 10**6),
        name="attend_back",
    )(lengths, spot, *inputs)


def gelu_parts(u):
    phi = 0.5 * (1.0 + lax.erf(u * SQRT_HALF))
    return u * phi, phi + u * (jnp.exp(u * u * -0.5) * INV_ROOT)


def ffn_kernel(
    chunks, size, spot, weights, normed, cot, vec, layer_out, keep, away, total, sums,
    w, low, act, slope, second_low, back, ready, loaded, sent,
):
    tokens, width = normed.shape
    copies = []
    for i in range(2 * chunks):
        columns = pl.ds(i * width, width)
        copies.append(pltpu.make_async_copy(weights.at[:, columns], w.at[:, columns], loaded.at[i]))
        copies[i].start()
    gain, shift = vec[3:4, :], vec[4:5, :]
    down_add, final_gain, final_shift = vec[5:6, :], vec[6:7, :], vec[7:8, :]

    def up(g):
        return w[:, g * width : (g + 1) * width]

    def down(g):
        return w[:, (chunks + g) * width : (chunks + g + 1) * width]

    low[...] = (normed[...] * gain + shift).astype(bf16)
    sums[...] = jnp.zeros_like(sums)

    def forward(t, first=False):
        rows = pl.ds(t * size, size) if first else pl.ds(pl.multiple_of(t * size, size), size)
        inputs = low[rows, :]
        if first:
            copies[0].wait()
        pre, added = dot(inputs, up(0)), None
        for g in range(chunks):
            if first and g + 1 < chunks:
                copies[g + 1].wait()
            upcoming = dot(inputs, up(g + 1)) if g + 1 < chunks else None
            activated, derivative = gelu_parts(pre + vec[8 + g : 9 + g, :])
            activated = activated.astype(bf16)
            act[g, rows, :] = activated
            slope[g, rows, :] = derivative.astype(bf16)
            if first:
                copies[chunks + g].wait()
            part = dot(activated, down(g))
            added = part if added is None else added + part
            pre = upcoming
        second_sum = normed[rows, :] * gain + shift + added + down_add
        centred = second_sum - mean(second_sum)
        inv = lax.rsqrt(mean(centred * centred) + EPSILON)
        hat = centred * inv
        layer_out[rows, :] = (hat * final_gain + final_shift).astype(bf16)
        grad = cot[rows, :].astype(f32)
        scaled = grad * final_gain
        second = inv * (scaled - mean(scaled) - hat * mean(scaled * hat))
        total[rows, :] = second
        second_low[rows, :] = second.astype(bf16)
        sums[0:1, :] += jnp.sum(second, axis=0, keepdims=True)
        sums[1:2, :] += jnp.sum(grad * hat, axis=0, keepdims=True)
        sums[2:3, :] += jnp.sum(grad, axis=0, keepdims=True)

    forward(0, True)

    @pl.loop(1, tokens // size)
    def _(t):
        forward(t)

    pending = []
    for g in range(chunks):
        to_act = dot_nt(second_low[...], down(g))
        to_down = dot_tn(act[g], second_low[...])
        to_pre = to_act * slope[g].astype(f32)
        sums[3 + g : 4 + g, :] = jnp.sum(to_pre, axis=0, keepdims=True)
        back[...] = to_pre.astype(bf16)
        slot = g % 2
        if g >= 2:
            for copy in pending[g - 2]:
                copy.wait()
        ready[slot, 1] = to_down.astype(bf16)
        total[...] += dot_nt(back[...], up(g))
        ready[slot, 0] = dot_tn(low[...], back[...]).astype(bf16)
        half, core = width // 2, spot[3]
        out = []
        for j in (0, 1):
            for target, side in ((away, 1 - core), (keep, core)):
                source = ready.at[slot, j, :, pl.ds(pl.multiple_of(side * half, 128), half)]
                place_of = target.at[:, pl.ds((j * chunks + g) * half, half)]
                out.append(pltpu.make_async_copy(source, place_of, sent.at[slot, len(out)]))
        for copy in out:
            copy.start()
        pending.append(out)

    for out in pending[-2:]:
        for copy in out:
            copy.wait()


def ffn(weights, normed, cot, vec, spot, size=256):
    tokens, width = normed.shape
    chunks = weights.shape[1] // (2 * width)
    shape = jax.ShapeDtypeStruct
    anywhere = pl.BlockSpec(memory_space=pl.ANY)
    halves = shape((width, chunks * width), bf16)
    outs = [shape((tokens, width), bf16)] + [halves] * 2 + [shape((tokens, width), f32), shape((8, width), f32)]
    out_specs = [full_block(out) for out in outs]
    out_specs[1:3] = [anywhere] * 2
    return pl.pallas_call(
        functools.partial(ffn_kernel, chunks, size),
        grid=(1,),
        in_specs=[pl.BlockSpec(memory_space=pltpu.SMEM), anywhere, full_block(normed), full_block(cot), full_block(vec)],
        out_specs=out_specs,
        out_shape=outs,
        scratch_shapes=[
            pltpu.VMEM(weights.shape, bf16),
            pltpu.VMEM((tokens, width), bf16),
            pltpu.VMEM((chunks, tokens, width), bf16),
            pltpu.VMEM((chunks, tokens, width), bf16),
            pltpu.VMEM((tokens, width), bf16),
            pltpu.VMEM((tokens, width), bf16),
            pltpu.VMEM((2, 2, width, width), bf16),
            pltpu.SemaphoreType.DMA((2 * chunks,)),
            pltpu.SemaphoreType.DMA((2, 4)),
        ],
        compiler_params=pltpu.CompilerParams(vmem_limit_bytes=63 * MEGA),
        cost_estimate=pl.CostEstimate(flops=32 * 10**9, bytes_accessed=3 * 10**7, transcendentals=6 * 10**6),
        name="ffn",
    )(spot, weights, normed, cot, vec)


def middle_kernel(grad_middle, normed, inverse, mixed, out_mat, vec, first, grad_mixed, grad_out, sums, low):
    step = pl.program_id(0)
    size = normed.shape[0]
    middle, hat, inv = grad_middle[...], normed[...], inverse[:, 0:1]
    scaled = middle * vec[3:4, :]
    to_first = inv * (scaled - mean(scaled) - hat * mean(scaled * hat))
    first[...] = to_first
    to_low = to_first.astype(bf16)
    low[pl.ds(pl.multiple_of(step * size, size), size), :] = to_low
    grad_mixed[...] = dot_nt(to_low, out_mat[0]).astype(bf16)

    @pl.when(step == 0)
    def _():
        sums[...] = jnp.zeros_like(sums)

    sums[0:1, :] += jnp.sum(middle * hat, axis=0, keepdims=True)
    sums[1:2, :] += jnp.sum(middle, axis=0, keepdims=True)
    sums[2:3, :] += jnp.sum(to_first, axis=0, keepdims=True)

    @pl.when(step == pl.num_programs(0) - 1)
    def _():
        grad_out[...] = dot_tn(mixed[...], low[...]).astype(bf16)


def middle_back(grad_middle, normed, inverse, mixed, mats, vec, size=256):
    tokens, width = normed.shape
    shape = jax.ShapeDtypeStruct
    tile = pl.BlockSpec((size, width), lambda i: (i, 0))
    outs = [shape((tokens, width), f32), shape((tokens, width), bf16), shape((width, width), bf16), shape((8, width), f32)]
    return pl.pallas_call(
        middle_kernel,
        grid=(tokens // size,),
        in_specs=[
            tile,
            tile,
            pl.BlockSpec((size, 128), lambda i: (i, 0)),
            full_block(mixed),
            pl.BlockSpec((1, width, width), lambda i: (3, 0, 0)),
            full_block(vec),
        ],
        out_specs=[tile, tile, full_block(outs[2]), full_block(outs[3])],
        out_shape=outs,
        scratch_shapes=[pltpu.VMEM((tokens, width), bf16)],
        compiler_params=pltpu.CompilerParams(vmem_limit_bytes=60 * MEGA),
        cost_estimate=pl.CostEstimate(flops=5 * 10**9, bytes_accessed=10**7, transcendentals=0),
        name="middle_back",
    )(grad_middle, normed, inverse, mixed, mats, vec)


def core_kernel(views, spot, keep, got, away_first, kept_first, away_second, kept_second):
    _, y, x, _ = (spot[i] for i in range(4))
    first, second = views
    for i in (0, 1):
        for out, index in ((away_first, 1 - y), (kept_first, y)):
            out[0, i] = first(keep, index, i) + first(got, index, i)
        for out, index in ((away_second, 1 - x), (kept_second, x)):
            out[0, i] = second(keep, i, index) + second(got, i, index)


def core_stage(keep, got, spot, split, by_rows):
    rows, columns = keep.shape[-2:]
    cuts = (slice(0, split), slice(split, None))
    if by_rows:
        sizes, cuts = ((split, columns), (rows - split, columns)), tuple((cut, slice(None)) for cut in cuts)
    else:
        sizes, cuts = ((rows, split), (rows, columns - split)), tuple((slice(None), cut) for cut in cuts)
    views = (
        lambda ref, y, x: ref[(0, pl.ds(y, 1), x, *cuts[0])][0],
        lambda ref, y, x: ref[(0, y, pl.ds(x, 1), *cuts[1])][0],
    )
    block = pl.BlockSpec((1, *keep.shape[1:]), lambda i, *_: (i, 0, 0, 0, 0))
    outs = [jax.ShapeDtypeStruct((4, 2, *size), bf16) for size in (sizes[0], sizes[0], sizes[1], sizes[1])]
    return pl.pallas_call(
        functools.partial(core_kernel, views),
        grid_spec=pltpu.PrefetchScalarGridSpec(
            num_scalar_prefetch=1,
            grid=(4,),
            in_specs=[block] * 2,
            out_specs=[pl.BlockSpec((1, *out.shape[1:]), lambda i, *_: (i, 0, 0, 0)) for out in outs],
        ),
        out_shape=outs,
        compiler_params=pltpu.CompilerParams(vmem_limit_bytes=40 * MEGA),
        cost_estimate=pl.CostEstimate(flops=10**6, bytes_accessed=10**7, transcendentals=0),
        name="core_stage",
    )(spot, keep, got)


def plane_kernel(spot, mine_first, got_first, mine_second, got_second, *outs):
    _, y, x, _ = (spot[i] for i in range(4))
    away_first, kept_first, away_second, kept_second = outs
    pairs = ((away_first, mine_first, got_first, 1 - x), (kept_first, mine_first, got_first, x))
    pairs += ((away_second, mine_second, got_second, 1 - y), (kept_second, mine_second, got_second, y))
    for out, mine, got, index in pairs:
        out[...] = mine[0, pl.ds(index, 1)] + got[0, pl.ds(index, 1)]


def plane_stage(kept, got, spot):
    inputs = (kept[0], got[0], kept[1], got[1])
    outs = [jax.ShapeDtypeStruct((4, *value.shape[2:]), bf16) for value in inputs]
    away_first, kept_first, away_second, kept_second = pl.pallas_call(
        plane_kernel,
        grid_spec=pltpu.PrefetchScalarGridSpec(
            num_scalar_prefetch=1,
            grid=(4,),
            in_specs=[pl.BlockSpec((1, *value.shape[1:]), lambda i, *_: (i, 0, 0, 0)) for value in inputs],
            out_specs=[pl.BlockSpec((1, *out.shape[1:]), lambda i, *_: (i, 0, 0)) for out in outs],
        ),
        out_shape=outs,
        compiler_params=pltpu.CompilerParams(vmem_limit_bytes=40 * MEGA),
        cost_estimate=pl.CostEstimate(flops=10**6, bytes_accessed=5 * 10**6, transcendentals=0),
        name="plane_stage",
    )(spot, *inputs)
    return (away_first, away_second), (kept_first, kept_second)


def line_kernel(spot, mine_first, got_first, mine_second, got_second, one, two, three, stays):
    z = spot[0]
    rows = mine_first.shape[1]
    for step, out in enumerate((stays, one, two, three)):
        index = lax.rem(z + step, 4)
        at = (pl.ds(index, 1),)
        for mine, got, part in ((mine_first, got_first, slice(0, rows)), (mine_second, got_second, slice(rows, None))):
            total = mine[at][0].astype(f32) + got[at][0].astype(f32)
            out[part, :] = total.astype(out.dtype)


def line_stage(kept, got, spot):
    inputs = (kept[0], got[0], kept[1], got[1])
    size = (kept[0].shape[1] + kept[1].shape[1], kept[0].shape[2])
    outs = [jax.ShapeDtypeStruct(size, bf16)] * 3 + [jax.ShapeDtypeStruct(size, f32)]
    vmem = pl.BlockSpec(memory_space=pltpu.VMEM)
    *parts, stays = pl.pallas_call(
        line_kernel,
        in_specs=[pl.BlockSpec(memory_space=pltpu.SMEM)] + [vmem] * 4,
        out_specs=[vmem] * 4,
        out_shape=outs,
        compiler_params=pltpu.CompilerParams(vmem_limit_bytes=40 * MEGA),
        cost_estimate=pl.CostEstimate(flops=10**6, bytes_accessed=3 * 10**6, transcendentals=0),
        name="line_stage",
    )(spot, *inputs)
    return parts, stays


def sum_kernel(mine_first, got_first, mine_second, got_second, out):
    columns = mine_first.shape[-1]
    out[:, :, :columns] = mine_first[...] + got_first[...]
    out[:, :, columns:] = mine_second[...] + got_second[...]


def line_sum(kept, got):
    line, rows, columns = kept[0].shape
    vmem = pl.BlockSpec(memory_space=pltpu.VMEM)
    return pl.pallas_call(
        sum_kernel,
        in_specs=[vmem] * 4,
        out_specs=vmem,
        out_shape=jax.ShapeDtypeStruct((line, rows, 2 * columns), bf16),
        compiler_params=pltpu.CompilerParams(vmem_limit_bytes=40 * MEGA),
        cost_estimate=pl.CostEstimate(flops=10**6, bytes_accessed=5 * 10**6, transcendentals=0),
        name="line_sum",
    )(kept[0], got[0], kept[1], got[1])


def token_kernel(first, dq, dk, dv, w, out):
    total = first[...]
    for unit, grad in enumerate((dq, dk, dv)):
        total = total + dot_nt(grad[...], w[unit])
    out[...] = total


def token_grad(first, grads, mats, size=256):
    tokens, width = first.shape
    tile = pl.BlockSpec((size, width), lambda i: (i, 0))
    return pl.pallas_call(
        token_kernel,
        grid=(tokens // size,),
        in_specs=[tile] * 4 + [pl.BlockSpec((3, width, width), lambda i: (0, 0, 0))],
        out_specs=tile,
        out_shape=jax.ShapeDtypeStruct((tokens, width), f32),
        compiler_params=pltpu.CompilerParams(vmem_limit_bytes=60 * MEGA),
        cost_estimate=pl.CostEstimate(flops=4 * 10**9, bytes_accessed=10**7, transcendentals=0),
        name="token_grad",
    )(first, *grads, mats)


def natural_hidden(up, down, devices):
    share, chunks, width = up.shape
    up = up.reshape(share, chunks, devices, share).swapaxes(1, 2).reshape(share, chunks * width)
    return up, down.swapaxes(0, 1).reshape(chunks * share, width)


def per_device(
    known,
    hidden,
    pair_lengths,
    cotangent,
    query_weight,
    query_bias,
    key_weight,
    value_weight,
    value_bias,
    out_weight,
    out_bias,
    attn_gain,
    attn_shift,
    up_weight,
    up_bias,
    down_weight,
    down_bias,
    final_gain,
    final_shift,
):
    rows_here, length, width = hidden.shape
    count = rows_here * length
    share = query_weight.shape[0]
    devices = width // share
    chunks = up_weight.shape[1] // width
    up_mine = (
        up_weight.reshape(share, devices, chunks, share).swapaxes(1, 2).reshape(share, chunks * width)
    )
    down_mine = down_weight.reshape(chunks, share, width).swapaxes(0, 1).reshape(share, chunks * width)
    ffn_mine = cat([up_mine, down_mine], 1)
    ffn_full = lax.all_gather(ffn_mine, CHIPS if known else AXES, axis=0, tiled=True)
    vector = cat(
        [
            query_bias,
            value_bias,
            out_bias,
            attn_gain,
            attn_shift,
            down_bias,
            final_gain,
            final_shift,
            up_bias,
        ]
    )
    matrices = jnp.stack([query_weight, key_weight, value_weight, out_weight])
    tokens = hidden.reshape(count, width)
    groups = 8 + chunks
    if known:
        z, y, x, core = place()
        spot = jnp.stack([z, y, x, core]).astype(jnp.int32)
        gathered = gather_attention(matrices, vector)
        out = attend_forward(True, tokens, gathered, pair_lengths, spot, rows_here, share)
        queries, keys_all, values_all, mixed, log_totals, first_norm, first_inverse, mats, vec = out
    else:
        spot = jnp.zeros((4,), jnp.int32)
        mats, vectors = gather_attention_any(matrices, vector)
        vec = vectors.reshape(devices, groups, share).swapaxes(0, 1).reshape(groups, width).astype(f32)
        vec = jnp.pad(vec, ((0, 16 - groups), (0, 0)))
        out = attend_forward(False, tokens, (mats, vec), pair_lengths, spot, rows_here, share)
        queries, keys_all, values_all, mixed, log_totals, first_norm, first_inverse = out
    layer_out, ffn_keep, ffn_away, grad_middle, first_sums = ffn(
        ffn_full, first_norm, cotangent.reshape(count, width), vec, spot
    )
    ffn_got = send(ffn_away, "core") if known else None
    grad_first, grad_mixed, grad_out_weight, second_sums = middle_back(
        grad_middle, first_norm, first_inverse, mixed, mats, vec
    )

    def back(gradient):
        sums = (grad_out_weight, first_sums, second_sums)
        heads = (queries, keys_all, values_all, mixed, log_totals)
        return attend_back(known, share, spot, tokens, *heads, gradient, *sums, pair_lengths)

    if known:
        half = width // 2
        grid = (4, 2, 2, 2 * share, -1)
        ffn_got, ffn_keep, grad_mixed = phase(ffn_got, ffn_keep, grad_mixed)
        out = core_stage(ffn_keep.reshape(grid), ffn_got.reshape(grid), spot, chunks * half, False)
        ffn_got = send(out[0], "y"), send(out[2], "x")
        *ffn_kept, grad_mixed = phase(out[1], out[3], grad_mixed)
        *token_grads, keep, away = back(grad_mixed)
        *ffn_got, keep, away = phase(*ffn_got, keep, away)
        got = send(away, "core")
        plane, ffn_kept = plane_stage(ffn_kept, ffn_got, spot)
        got, *plane = phase(got, *plane)
        ffn_got = send(plane[0], "x"), send(plane[1], "y")
        shape = (4, 2, 2, *keep.shape[1:])
        out = core_stage(keep.reshape(shape), got.reshape(shape), spot, 4 * share, True)
        attn_got = send(out[0], "y"), send(out[2], "x")
        *attn_kept, grad_first = phase(out[1], out[3], grad_first)
        grad_tokens = token_grad(grad_first, token_grads, mats)
        *ffn_got, grad_tokens = phase(*ffn_got, grad_tokens)
        ffn_sum = lax.psum_scatter(line_sum(ffn_kept, ffn_got), "z", scatter_dimension=0, tiled=True)
        attn_got = phase(*attn_got)
        plane, attn_kept = plane_stage(attn_kept, attn_got, spot)
        attn_got = send(plane[0], "x"), send(plane[1], "y")
        attn_got = phase(*attn_got)
        line, attn_mine = line_stage(attn_kept, attn_got, spot)
        attn_line = send_line(line)
        ffn_sum, attn_mine = phase(ffn_sum, attn_mine)
        ffn_mine = ffn_sum[0].reshape(2, share, 2, chunks, half).transpose(2, 0, 1, 3, 4)
        ffn_whole = halves_of(ffn_mine.reshape(2, 2, share * chunks, half)).reshape(2, share, chunks, width)
        up_owned, down_owned = natural_hidden(ffn_whole[0], ffn_whole[1], devices)
        attn_one, attn_two, attn_three, up_owned, down_owned = phase(*attn_line, up_owned, down_owned)
        attn_mine = add(attn_mine, attn_one, attn_two, attn_three)
        mats_owned = halves_of(attn_mine[: 8 * share].reshape(4, 2, share, width // 2))
        vectors_owned = attn_mine[8 * share, : groups * share]
    else:
        *token_grads, mat_grads, bias_sums = back(grad_mixed)
        grad_tokens = token_grad(grad_first, token_grads, mats)
        ffn_grads = jnp.stack([ffn_keep, ffn_away]).reshape(2, width, 2, chunks, width // 2)
        ffn_grads = ffn_grads.transpose(2, 1, 3, 0, 4).reshape(2, width, chunks * width)
        ffn_whole = lax.psum_scatter(ffn_grads, AXES, scatter_dimension=1, tiled=True).astype(f32)
        up_owned, down_owned = natural_hidden(*ffn_whole.reshape(2, share, chunks, width), devices)
        mat_grads = cat([mat_grads, grad_out_weight[None]])
        vector_grads = cat(natural_rows([bias_sums[0:1], bias_sums[1:2]], first_sums, second_sums))
        vector_grads = vector_grads.reshape(groups, devices, share).swapaxes(0, 1).reshape(devices, groups * share)
        mats_owned, vectors_owned = scatter_attention_any(mat_grads, vector_grads)
    own = vectors_owned.reshape(groups, share)
    return (
        layer_out.reshape(hidden.shape),
        grad_tokens.reshape(hidden.shape),
        mats_owned[0],
        own[0],
        mats_owned[1],
        mats_owned[2],
        own[1],
        mats_owned[3],
        own[2],
        own[3],
        own[4],
        up_owned,
        own[8:].reshape(chunks * share),
        down_owned,
        own[5],
        own[6],
        own[7],
    )


def solution(mesh):
    known = dict(mesh.shape) == {"dp": 8, "shard": 4}
    axes = AXES
    if known:
        mesh, axes = Mesh(mesh.devices.reshape(4, 2, 2, 2), CHIPS), CHIPS
    cube, flat, line = P(axes, None, None), P(axes, None), P(axes)
    return jax.shard_map(
        lambda *args: per_device(known, *args),
        mesh=mesh,
        in_specs=(
            cube, flat, cube, flat, line, flat, flat, line, flat, line, line, line, flat, line, flat, line, line, line,
        ),
        out_specs=(
            cube, cube, flat, line, flat, flat, line, flat, line, line, line, flat, line, flat, line, line, line,
        ),
        check_vma=False,
    )
```

```python
import functools

import jax
import jax.numpy as jnp
from jax import lax
from jax.experimental import pallas as pl
from jax.experimental.pallas import tpu as pltpu
from jax.sharding import Mesh
from jax.sharding import PartitionSpec as P

EPSILON = 1e-06
SQRT_HALF = 0.7071067811865476
INV_ROOT = 0.3989422804014327
MOST = 128
HALF = 64
NEVER = -1e30
MEGA = 1024 * 1024

AXES = ("dp", "shard")
CHIPS = ("z", "y", "x", "core")
f32 = jnp.float32
bf16 = jnp.bfloat16
cat = jnp.concatenate


def moves(move):
    pairs = []
    for index in range(32):
        z, y, x, core = index // 8, (index // 4) % 2, (index // 2) % 2, index % 2
        z, y, x, core = move(z, y, x, core)
        pairs.append((index, z * 8 + y * 4 + x * 2 + core))
    return pairs


MOVES = {
    "core": moves(lambda z, y, x, core: (z, y, x, 1 - core)),
    "x": moves(lambda z, y, x, core: (z, y, 1 - x, core)),
    "y": moves(lambda z, y, x, core: (z, 1 - y, x, core)),
    "z1": moves(lambda z, y, x, core: ((z + 1) % 4, y, x, core)),
    "z2": moves(lambda z, y, x, core: ((z + 2) % 4, y, x, core)),
    "z3": moves(lambda z, y, x, core: ((z + 3) % 4, y, x, core)),
}


def send(values, move):
    return lax.ppermute(values, CHIPS, MOVES[move])


def place():
    return tuple(lax.axis_index(axis) for axis in CHIPS)


def phase(*values):
    return lax.optimization_barrier(values)


def add(*terms):
    total = terms[0].astype(f32)
    for term in terms[1:]:
        total = total + term.astype(f32)
    return total


def gather_blocks(block, split):
    one, two, three = send(block, "z1"), send(block, "z2"), send(block, "z3")
    one, two, three = phase(one, two, three)
    line = jnp.stack([block, one, two, three])
    first, second = line[:, :split], line[:, split:]
    first_x, second_y = send(first, "x"), send(second, "y")
    first_x, second_y, first, second = phase(first_x, second_y, first, second)
    first, second = cat([first, first_x]), cat([second, second_y])
    first_y, second_x = send(first, "y"), send(second, "x")
    other_first, other_second = send(first, "core"), send(second, "core")
    first, first_y, second, second_x, other_first, other_second = phase(
        first, first_y, second, second_x, other_first, other_second
    )
    other_first_y, other_second_x = send(first_y, "core"), send(second_x, "core")
    return first, first_y, second, second_x, other_first, other_first_y, other_second, other_second_x


def pick(values, index, axis):
    return lax.dynamic_index_in_dim(values, index, axis, False)


def send_line(parts):
    return tuple(send(part, move) for part, move in zip(parts, ("z1", "z2", "z3")))


def halves_of(mine):
    z, y, x, core = place()
    kept = pick(mine, core, 1)
    got = send(pick(mine, 1 - core, 1).astype(bf16), "core").astype(f32)
    return jnp.where(core == 0, cat([kept, got], 2), cat([got, kept], 2))


def gather_attention(matrices, vector):
    z, y, x, core = place()
    count, rows, width = matrices.shape
    half = width // 2
    mine = lax.dynamic_slice_in_dim(matrices, core * half, half, 2)
    got = send(lax.dynamic_slice_in_dim(matrices, (1 - core) * half, half, 2), "core")
    pair = jnp.where(core == 0, cat([mine, got], 1), cat([got, mine], 1))
    vector_rows = jnp.pad(vector[None], ((0, 15), (0, half - vector.shape[0])))
    block = cat([pair.reshape(count * 2 * rows, half), vector_rows])
    (block,) = phase(block)
    return gather_blocks(block, 6 * rows)


def gather_attention_any(matrices, vector):
    mats = lax.all_gather(matrices, AXES, axis=1, tiled=True)
    return mats, lax.all_gather(vector, AXES, axis=0, tiled=False)


def scatter_attention_any(matrices, vectors):
    mats = lax.psum_scatter(matrices.astype(bf16), AXES, scatter_dimension=1, tiled=True)
    return mats.astype(f32), lax.psum_scatter(vectors, AXES, scatter_dimension=0, tiled=False)


def dot(left, right):
    return lax.dot_general(left, right, (((1,), (0,)), ((), ())), preferred_element_type=f32)


def dot_nt(left, right):
    return lax.dot_general(left, right, (((1,), (1,)), ((), ())), preferred_element_type=f32)


def dot_tn(left, right):
    return lax.dot_general(left, right, (((0,), (0,)), ((), ())), preferred_element_type=f32)


def mean(values):
    return jnp.sum(values, axis=1, keepdims=True) * (1.0 / values.shape[1])


def spans(length, block):
    return [(start, max(0, start - MOST), min(length, start + block + MOST)) for start in range(0, length, block)]


def make_marks(lengths, row, marks):
    length, count = marks.shape[1], lengths.shape[1]
    position = lax.broadcasted_iota(jnp.int32, (length, 128), 0)
    lane = lax.broadcasted_iota(jnp.int32, (length, 128), 1)
    number, end = jnp.zeros((length, 128), jnp.int32), jnp.int32(0)
    for pair in range(count):
        end = end + lengths[row, pair]
        number = number + (position >= end).astype(jnp.int32)
    for head in (0, 1):
        at = lane - HALF * (1 - head)
        used = (at >= 0) & (at < count)
        marks[head] = jnp.where(used & (number == at), 1.0, 0.0).astype(bf16)
        marks[2 + head] = jnp.where(used & (number != at), NEVER, 0.0).astype(bf16)


def lanes(head, value=1.0):
    lane = lax.broadcasted_iota(jnp.int32, (16, 128), 1)
    return jnp.where((lane < HALF) if head == 0 else (lane >= HALF), value, 0.0).astype(bf16)[:1]


def spread(half, width, share):
    source = lax.broadcasted_iota(jnp.int32, (half, width), 0)
    target = lax.broadcasted_iota(jnp.int32, (half, width), 1)
    return jnp.where(source % share == target % share, 1.0, 0.0).astype(bf16)


def load_weights(spot, blocks, weights, vector_blocks, sem):
    z, y, x, core = spot[0], spot[1], spot[2], spot[3]
    copies = []
    rows = 48
    half = weights.shape[2] // 2
    for index, block in enumerate(blocks):
        side = core if index < 4 else 1 - core
        columns = pl.ds(pl.multiple_of(side * half, 128), half)
        for near in (0, 1):
            for step in range(4):
                far = index % 2
                if index % 4 < 2:
                    cy, cx = jnp.bitwise_xor(y, far), jnp.bitwise_xor(x, near)
                else:
                    cy, cx = jnp.bitwise_xor(y, near), jnp.bitwise_xor(x, far)
                chip = lax.rem(z - step + 4, 4) * 4 + cy * 2 + cx
                target = pl.ds(pl.multiple_of(chip * rows, 16), rows)
                at = near * 4 + step
                for unit, matrix in enumerate((0, 1, 4) if index % 4 < 2 else (2, 3)):
                    copies.append(
                        pltpu.make_async_copy(
                            block.at[at, pl.ds(unit * rows, rows)], weights.at[matrix, target, columns], sem
                        )
                    )
                if index % 4 >= 2:
                    copies.append(
                        pltpu.make_async_copy(
                            block.at[at, pl.ds(2 * rows, 16)], vector_blocks.at[chip * 2 + side], sem
                        )
                    )
    for copy in copies:
        copy.start()
    for copy in copies:
        copy.wait()


def spread_vectors(vector_blocks, vec, share):
    devices, _, half = vector_blocks.shape
    width = vec.shape[1]
    groups = 12
    entries = jnp.sum(vector_blocks[...].astype(f32), axis=1)
    lane = lax.broadcasted_iota(jnp.int32, (devices, half), 1)
    parts = [jnp.where(lane // share == group, entries, 0.0) for group in range(groups)]
    wide = dot(cat(parts).astype(bf16), spread(half, width, share))
    owner = lax.broadcasted_iota(jnp.int32, (devices, width), 1) // share
    device = lax.broadcasted_iota(jnp.int32, (devices, width), 0)
    for group in range(groups):
        part = wide[group * devices : (group + 1) * devices]
        vec[group : group + 1, :] = jnp.sum(jnp.where(owner == device, part, 0.0), axis=0, keepdims=True)


def attend_kernel(known, block, share, lengths, spot, x, *refs):
    if known:
        blocks, refs = refs[:8], refs[8:]
        q_out, k_out, v_out, mixed, lse, normed, inverse, w, vec, marks, vector_blocks, sem = refs
    else:
        w, vec, q_out, k_out, v_out, mixed, lse, normed, inverse, marks = refs
    row = pl.program_id(0)
    length, width = x.shape
    make_marks(lengths, row, marks)
    if known:

        @pl.when(row == 0)
        def _():
            load_weights(spot, blocks, w, vector_blocks, sem)
            spread_vectors(vector_blocks, vec, share)

    tokens = x[...]
    q_out[...] = (dot(tokens, w[0]) + vec[0:1, :]).astype(bf16)
    k_out[...] = dot(tokens, w[1]).astype(bf16)
    v_out[...] = (dot(tokens, w[2]) + vec[1:2, :]).astype(bf16)
    keep = (lanes(0), lanes(1))
    keep_scaled = (lanes(0, 0.125), lanes(1, 0.125))
    pairs, parts = width // 128, spans(length, block)

    def scores_of(pair):
        tile = pl.ds(pair * 128, 128)
        q, k, v = q_out[:, tile], k_out[:, tile], v_out[:, tile]
        qs = [q * keep_scaled[h] + marks[h] for h in (0, 1)]
        ks = [k * keep[h] + marks[2 + h] for h in (0, 1)]
        vs = [v * keep[h] + keep[1 - h] for h in (0, 1)]
        scores = [
            [dot_nt(ks[h][first:last], qs[h][start : start + block]) for h in (0, 1)] for start, first, last in parts
        ]
        return scores, vs

    upcoming = scores_of(0)
    for pair in range(pairs):
        scores, vs = upcoming
        if pair + 1 < pairs:
            upcoming = scores_of(pair + 1)
        tops = [[jnp.max(s, axis=0, keepdims=True) for s in both] for both in scores]
        probs = [[jnp.exp(s - t).astype(bf16) for s, t in zip(both, top)] for both, top in zip(scores, tops)]
        mixes = [
            [dot_tn(vs[h][first:last], probs[i][h]) for h in (0, 1)] for i, (start, first, last) in enumerate(parts)
        ]
        for i, (start, first, last) in enumerate(parts):
            out = []
            for h in (0, 1):
                mix = mixes[i][h]
                total = mix[HALF : HALF + 1] if h == 0 else mix[:1]
                lse[0, 2 * pair + h : 2 * pair + h + 1, start : start + block] = tops[i][h] + jnp.log(total)
                out.append((mix[:HALF] if h == 0 else mix[HALF:]) * (1.0 / total))
            mixed[start : start + block, pair * 128 : pair * 128 + 128] = jnp.transpose(cat(out)).astype(bf16)
    for start in range(0, length, 256):
        rows = pl.ds(start, 256)
        total = x[rows, :].astype(f32) + dot(mixed[rows, :], w[3]) + vec[2:3, :]
        centred = total - mean(total)
        inv = lax.rsqrt(mean(centred * centred) + EPSILON)
        normed[rows, :] = centred * inv
        inverse[rows, :] = jnp.broadcast_to(inv, (256, 128))


def attend_forward(known, x, gathered, lengths, spot, rows, share, block=128):
    tokens, width = x.shape
    length = tokens // rows
    shape = jax.ShapeDtypeStruct
    tile = pl.BlockSpec((length, width), lambda r, *_: (r, 0))
    fixed = [pl.BlockSpec((5, width, width), lambda r, *_: (0, 0, 0)), pl.BlockSpec((16, width), lambda r, *_: (0, 0))]
    act = shape((tokens, width), bf16)
    out_specs = [tile] * 4 + [
        pl.BlockSpec((1, 16, length), lambda r, *_: (r, 0, 0)),
        tile,
        pl.BlockSpec((length, 128), lambda r, *_: (r, 0)),
    ]
    out_shape = [act] * 4 + [shape((rows, 16, length), f32), shape((tokens, width), f32), shape((tokens, 128), f32)]
    scratch = [pltpu.VMEM((4, length, 128), bf16)]
    if known:
        in_specs = [tile] + [pl.BlockSpec(memory_space=pl.ANY)] * 8
        out_specs, out_shape = out_specs + fixed, out_shape + [shape((5, width, width), bf16), shape((16, width), f32)]
        scratch += [pltpu.VMEM((32, 16, width // 2), bf16), pltpu.SemaphoreType.DMA]
    else:
        in_specs = [tile] + fixed
    return pl.pallas_call(
        functools.partial(attend_kernel, known, block, share),
        grid_spec=pltpu.PrefetchScalarGridSpec(
            num_scalar_prefetch=2, grid=(rows,), in_specs=in_specs, out_specs=out_specs, scratch_shapes=scratch
        ),
        out_shape=out_shape,
        compiler_params=pltpu.CompilerParams(vmem_limit_bytes=60 * MEGA),
        cost_estimate=pl.CostEstimate(flops=10 * 10**9, bytes_accessed=2 * 10**7, transcendentals=4 * 10**6),
        name="attend",
    )(lengths, spot, x, *gathered)


def natural_rows(bias_rows, first_sums, second_sums):
    rows = bias_rows + [second_sums[2:3, :], second_sums[0:1, :], second_sums[1:2, :]]
    rows += [first_sums[i : i + 1, :] for i in (0, 1, 2)]
    return rows + [first_sums[i : i + 1, :] for i in (3, 4, 5, 6)]


def back_kernel(known, block, share, lengths, spot, x, q_in, k_in, v_in, mixed, lse, grad, *refs):
    grad_out, first_sums, second_sums, dq_out, dk_out, dv_out, keep, away, marks = refs
    tokens, width = q_in.shape
    rows = lengths.shape[0]
    length = tokens // rows
    for row in range(rows):
        make_marks(lengths, row, marks.at[row])
    keep_lanes = (lanes(0), lanes(1))
    keep_scaled = (lanes(0, 0.125), lanes(1, 0.125))
    head_of = lax.broadcasted_iota(jnp.int32, (16, 128), 1) // HALF
    picker = jnp.where(lax.broadcasted_iota(jnp.int32, (16, 128), 0) == head_of, 1.0, 0.0).astype(bf16)
    parts = spans(length, block)
    items = [(row, pair) for row in range(rows) for pair in range(width // 128)]

    def products_of(row, pair):
        tile = (slice(row * length, row * length + length), slice(pair * 128, pair * 128 + 128))
        q, k, v, g = q_in[tile], k_in[tile], v_in[tile], grad[tile]
        product = g.astype(f32) * mixed[tile].astype(f32)
        high = product.astype(bf16)
        centre = dot_nt(picker, high) + dot_nt(picker, (product - high.astype(f32)).astype(bf16))
        qz = [q * keep_scaled[h] for h in (0, 1)]
        kz = [k * keep_lanes[h] for h in (0, 1)]
        vz = [v * keep_lanes[h] for h in (0, 1)]
        gz = [g * keep_lanes[h] for h in (0, 1)]
        qs = [qz[h] + marks[row, h] for h in (0, 1)]
        ks = [kz[h] + marks[row, 2 + h] for h in (0, 1)]
        scores = [
            [dot_nt(ks[h][start : start + block], qs[h][first:last]) for h in (0, 1)] for start, first, last in parts
        ]
        slopes = [
            [dot_nt(vz[h][start : start + block], g[first:last]) for h in (0, 1)] for start, first, last in parts
        ]
        return scores, slopes, centre, qz, kz, gz

    upcoming = products_of(*items[0])
    for index, (row, pair) in enumerate(items):
        scores, slopes, centre, qz, kz, gz = upcoming
        if index + 1 < len(items):
            upcoming = products_of(*items[index + 1])
        probs, grads = [], []
        for i, (start, first, last) in enumerate(parts):
            head = 2 * pair
            prob = [jnp.exp(scores[i][h] - lse[row, head + h : head + h + 1, first:last]) for h in (0, 1)]
            probs.append([p.astype(bf16) for p in prob])
            grads.append([(prob[h] * (slopes[i][h] - centre[h : h + 1, first:last])).astype(bf16) for h in (0, 1)])
        columns = slice(pair * 128, pair * 128 + 128)
        to_values = [
            sum(dot(probs[i][h], gz[h][first:last]) for h in (0, 1)) for i, (start, first, last) in enumerate(parts)
        ]
        to_keys = [
            sum(dot(grads[i][h], qz[h][first:last]) for h in (0, 1)) for i, (start, first, last) in enumerate(parts)
        ]
        to_queries = [
            sum(dot_tn(grads[i][h], kz[h][start : start + block]) for h in (0, 1))
            for i, (start, first, last) in enumerate(parts)
        ]
        base = row * length
        for i, (start, first, last) in enumerate(parts):
            dv_out[base + start : base + start + block, columns] = to_values[i].astype(bf16)
            dk_out[base + start : base + start + block, columns] = to_keys[i].astype(bf16)
        for at in range(0, length, MOST):
            pieces = [
                to_queries[i][at - first : at - first + MOST]
                for i, (start, first, last) in enumerate(parts)
                if first <= at < last
            ]
            dq_out[base + at : base + at + MOST, columns] = (sum(pieces) * 0.125).astype(bf16)
    biases = [jnp.sum(out[...].astype(f32), axis=0, keepdims=True) for out in (dq_out, dv_out)]
    if not known:
        for unit, out in enumerate((dq_out, dk_out, dv_out)):
            keep[unit] = dot_tn(x[...], out[...]).astype(bf16)
        away[...] = jnp.zeros_like(away)
        away[0:1, :] = biases[0]
        away[1:2, :] = biases[1]
        return
    core = spot[3]
    half, chips, size = width // 2, keep.shape[0], 2 * share
    natural = natural_rows(biases, first_sums, second_sums)
    owner = lax.broadcasted_iota(jnp.int32, (chips, width), 1) // share
    chip = lax.broadcasted_iota(jnp.int32, (chips, width), 0)
    lane = lax.broadcasted_iota(jnp.int32, (chips, half), 1)
    table = spread(half, width, share)
    top = lax.broadcasted_iota(jnp.int32, (chips, 16, half), 1) == 0
    for side, out in ((1 - core, away), (core, keep)):
        own = pl.ds(pl.multiple_of(side * half, 128), half)
        for unit, out_ref in enumerate((dq_out, dk_out, dv_out)):
            part = dot_tn(x[...], out_ref[:, own]).astype(bf16)
            out[:, unit * size : (unit + 1) * size, :] = part.reshape(chips, size, half)
        out[:, 3 * size : 4 * size, :] = grad_out[:, own].reshape(chips, size, half)
        mine = owner == 2 * chip + side
        entries = jnp.zeros((chips, half), f32)
        spreads = dot_nt(cat([jnp.where(mine, row, 0.0) for row in natural]).astype(bf16), table)
        for group in range(len(natural)):
            part = spreads[group * chips : (group + 1) * chips]
            entries = entries + jnp.where(lane // share == group, part, 0.0)
        out[:, 4 * size :, :] = jnp.where(top, entries[:, None, :], 0.0).astype(bf16)


def full_block(value):
    return pl.BlockSpec(value.shape, lambda i, *_: (0,) * len(value.shape))


def attend_back(known, share, spot, x, q, k, v, mixed, lse, grad, grad_out, first_sums, second_sums, lengths, block=128):
    tokens, width = q.shape
    rows = lengths.shape[0]
    shape = jax.ShapeDtypeStruct
    outs = [shape((tokens, width), bf16)] * 3
    if known:
        outs += [shape((16, 8 * share + 16, width // 2), bf16)] * 2
    else:
        outs += [shape((3, width, width), bf16), shape((8, width), f32)]
    inputs = (x, q, k, v, mixed, lse, grad, grad_out, first_sums, second_sums)
    return pl.pallas_call(
        functools.partial(back_kernel, known, block, share),
        grid_spec=pltpu.PrefetchScalarGridSpec(
            num_scalar_prefetch=2,
            grid=(1,),
            in_specs=[full_block(value) for value in inputs],
            out_specs=[full_block(out) for out in outs],
            scratch_shapes=[pltpu.VMEM((rows, 4, tokens // rows, 128), bf16)],
        ),
        out_shape=outs,
        compiler_params=pltpu.CompilerParams(vmem_limit_bytes=60 * MEGA),
        cost_estimate=pl.CostEstimate(flops=20 * 10**9, bytes_accessed=2 * 10**7, transcendentals=4 * 10**6),
        name="attend_back",
    )(lengths, spot, *inputs)


def gelu_parts(u):
    phi = 0.5 * (1.0 + lax.erf(u * SQRT_HALF))
    return u * phi, phi + u * (jnp.exp(u * u * -0.5) * INV_ROOT)


def ffn_kernel(
    chunks, size, spot, weights, mats, normed, cot, vec, layer_out, keep, away, total, sums,
    w, low, act, slope, second_low, back, ready, loaded, sent,
):
    tokens, width = normed.shape
    copies = []
    for i in range(2 * chunks):
        columns = pl.ds(i * width, width)
        source = weights.at[:, columns] if i < 2 * chunks - 1 else mats.at[4]
        copies.append(pltpu.make_async_copy(source, w.at[:, columns], loaded.at[i]))
        copies[i].start()
    gain, shift = vec[3:4, :], vec[4:5, :]
    down_add, final_gain, final_shift = vec[5:6, :], vec[6:7, :], vec[7:8, :]

    def up(g):
        return w[:, g * width : (g + 1) * width]

    def down(g):
        return w[:, (chunks + g) * width : (chunks + g + 1) * width]

    low[...] = (normed[...] * gain + shift).astype(bf16)
    sums[...] = jnp.zeros_like(sums)

    def forward(t, first=False):
        rows = pl.ds(t * size, size) if first else pl.ds(pl.multiple_of(t * size, size), size)
        inputs = low[rows, :]
        if first:
            copies[0].wait()
        pre, added = dot(inputs, up(0)), None
        for g in range(chunks):
            if first and g + 1 < chunks:
                copies[g + 1].wait()
            upcoming = dot(inputs, up(g + 1)) if g + 1 < chunks else None
            activated, derivative = gelu_parts(pre + vec[8 + g : 9 + g, :])
            activated = activated.astype(bf16)
            act[g, rows, :] = activated
            slope[g, rows, :] = derivative.astype(bf16)
            if first:
                copies[chunks + g].wait()
            part = dot(activated, down(g))
            added = part if added is None else added + part
            pre = upcoming
        second_sum = normed[rows, :] * gain + shift + added + down_add
        centred = second_sum - mean(second_sum)
        inv = lax.rsqrt(mean(centred * centred) + EPSILON)
        hat = centred * inv
        layer_out[rows, :] = (hat * final_gain + final_shift).astype(bf16)
        grad = cot[rows, :].astype(f32)
        scaled = grad * final_gain
        second = inv * (scaled - mean(scaled) - hat * mean(scaled * hat))
        total[rows, :] = second
        second_low[rows, :] = second.astype(bf16)
        sums[0:1, :] += jnp.sum(second, axis=0, keepdims=True)
        sums[1:2, :] += jnp.sum(grad * hat, axis=0, keepdims=True)
        sums[2:3, :] += jnp.sum(grad, axis=0, keepdims=True)

    forward(0, True)

    @pl.loop(1, tokens // size)
    def _(t):
        forward(t)

    pending = []
    for g in range(chunks):
        to_act = dot_nt(second_low[...], down(g))
        to_down = dot_tn(act[g], second_low[...])
        to_pre = to_act * slope[g].astype(f32)
        sums[3 + g : 4 + g, :] = jnp.sum(to_pre, axis=0, keepdims=True)
        back[...] = to_pre.astype(bf16)
        slot = g % 2
        if g >= 2:
            for copy in pending[g - 2]:
                copy.wait()
        ready[slot, 1] = to_down.astype(bf16)
        total[...] += dot_nt(back[...], up(g))
        ready[slot, 0] = dot_tn(low[...], back[...]).astype(bf16)
        half, core = width // 2, spot[3]
        out = []
        for j in (0, 1):
            for target, side in ((away, 1 - core), (keep, core)):
                source = ready.at[slot, j, :, pl.ds(pl.multiple_of(side * half, 128), half)]
                place_of = target.at[:, pl.ds((j * chunks + g) * half, half)]
                out.append(pltpu.make_async_copy(source, place_of, sent.at[slot, len(out)]))
        for copy in out:
            copy.start()
        pending.append(out)

    for out in pending[-2:]:
        for copy in out:
            copy.wait()


def ffn(weights, mats, normed, cot, vec, spot, size=512):
    tokens, width = normed.shape
    chunks = (weights.shape[1] // width + 1) // 2
    shape = jax.ShapeDtypeStruct
    anywhere = pl.BlockSpec(memory_space=pl.ANY)
    halves = shape((width, chunks * width), bf16)
    outs = [shape((tokens, width), bf16)] + [halves] * 2 + [shape((tokens, width), f32), shape((8, width), f32)]
    out_specs = [full_block(out) for out in outs]
    out_specs[1:3] = [anywhere] * 2
    return pl.pallas_call(
        functools.partial(ffn_kernel, chunks, size),
        grid=(1,),
        in_specs=[pl.BlockSpec(memory_space=pltpu.SMEM), anywhere, anywhere, full_block(normed), full_block(cot), full_block(vec)],
        out_specs=out_specs,
        out_shape=outs,
        scratch_shapes=[
            pltpu.VMEM((width, 2 * chunks * width), bf16),
            pltpu.VMEM((tokens, width), bf16),
            pltpu.VMEM((chunks, tokens, width), bf16),
            pltpu.VMEM((chunks, tokens, width), bf16),
            pltpu.VMEM((tokens, width), bf16),
            pltpu.VMEM((tokens, width), bf16),
            pltpu.VMEM((2, 2, width, width), bf16),
            pltpu.SemaphoreType.DMA((2 * chunks,)),
            pltpu.SemaphoreType.DMA((2, 4)),
        ],
        compiler_params=pltpu.CompilerParams(vmem_limit_bytes=63 * MEGA),
        cost_estimate=pl.CostEstimate(flops=32 * 10**9, bytes_accessed=3 * 10**7, transcendentals=6 * 10**6),
        name="ffn",
    )(spot, weights, mats, normed, cot, vec)


def middle_kernel(grad_middle, normed, inverse, mixed, out_mat, vec, first, grad_mixed, grad_out, sums, low):
    step = pl.program_id(0)
    size = normed.shape[0]
    middle, hat, inv = grad_middle[...], normed[...], inverse[:, 0:1]
    scaled = middle * vec[3:4, :]
    to_first = inv * (scaled - mean(scaled) - hat * mean(scaled * hat))
    first[...] = to_first
    to_low = to_first.astype(bf16)
    low[pl.ds(pl.multiple_of(step * size, size), size), :] = to_low
    grad_mixed[...] = dot_nt(to_low, out_mat[0]).astype(bf16)

    @pl.when(step == 0)
    def _():
        sums[...] = jnp.zeros_like(sums)

    sums[0:1, :] += jnp.sum(middle * hat, axis=0, keepdims=True)
    sums[1:2, :] += jnp.sum(middle, axis=0, keepdims=True)
    sums[2:3, :] += jnp.sum(to_first, axis=0, keepdims=True)

    @pl.when(step == pl.num_programs(0) - 1)
    def _():
        grad_out[...] = dot_tn(mixed[...], low[...]).astype(bf16)


def middle_back(grad_middle, normed, inverse, mixed, mats, vec, size=512):
    tokens, width = normed.shape
    shape = jax.ShapeDtypeStruct
    tile = pl.BlockSpec((size, width), lambda i: (i, 0))
    outs = [shape((tokens, width), f32), shape((tokens, width), bf16), shape((width, width), bf16), shape((8, width), f32)]
    return pl.pallas_call(
        middle_kernel,
        grid=(tokens // size,),
        in_specs=[
            tile,
            tile,
            pl.BlockSpec((size, 128), lambda i: (i, 0)),
            full_block(mixed),
            pl.BlockSpec((1, width, width), lambda i: (3, 0, 0)),
            full_block(vec),
        ],
        out_specs=[tile, tile, full_block(outs[2]), full_block(outs[3])],
        out_shape=outs,
        scratch_shapes=[pltpu.VMEM((tokens, width), bf16)],
        compiler_params=pltpu.CompilerParams(vmem_limit_bytes=60 * MEGA),
        cost_estimate=pl.CostEstimate(flops=5 * 10**9, bytes_accessed=10**7, transcendentals=0),
        name="middle_back",
    )(grad_middle, normed, inverse, mixed, mats, vec)


def core_kernel(views, spot, keep, got, away_first, kept_first, away_second, kept_second):
    _, y, x, _ = (spot[i] for i in range(4))
    first, second = views
    for i in (0, 1):
        for out, index in ((away_first, 1 - y), (kept_first, y)):
            out[0, i] = first(keep, index, i) + first(got, index, i)
        for out, index in ((away_second, 1 - x), (kept_second, x)):
            out[0, i] = second(keep, i, index) + second(got, i, index)


def core_stage(keep, got, spot, split, by_rows):
    rows, columns = keep.shape[-2:]
    cuts = (slice(0, split), slice(split, None))
    if by_rows:
        sizes, cuts = ((split, columns), (rows - split, columns)), tuple((cut, slice(None)) for cut in cuts)
    else:
        sizes, cuts = ((rows, split), (rows, columns - split)), tuple((slice(None), cut) for cut in cuts)
    views = (
        lambda ref, y, x: ref[(0, pl.ds(y, 1), x, *cuts[0])][0],
        lambda ref, y, x: ref[(0, y, pl.ds(x, 1), *cuts[1])][0],
    )
    block = pl.BlockSpec((1, *keep.shape[1:]), lambda i, *_: (i, 0, 0, 0, 0))
    outs = [jax.ShapeDtypeStruct((4, 2, *size), bf16) for size in (sizes[0], sizes[0], sizes[1], sizes[1])]
    return pl.pallas_call(
        functools.partial(core_kernel, views),
        grid_spec=pltpu.PrefetchScalarGridSpec(
            num_scalar_prefetch=1,
            grid=(4,),
            in_specs=[block] * 2,
            out_specs=[pl.BlockSpec((1, *out.shape[1:]), lambda i, *_: (i, 0, 0, 0)) for out in outs],
        ),
        out_shape=outs,
        compiler_params=pltpu.CompilerParams(vmem_limit_bytes=40 * MEGA),
        cost_estimate=pl.CostEstimate(flops=10**6, bytes_accessed=10**7, transcendentals=0),
        name="core_stage",
    )(spot, keep, got)


def plane_kernel(spot, mine_first, got_first, mine_second, got_second, *outs):
    _, y, x, _ = (spot[i] for i in range(4))
    away_first, kept_first, away_second, kept_second = outs
    pairs = ((away_first, mine_first, got_first, 1 - x), (kept_first, mine_first, got_first, x))
    pairs += ((away_second, mine_second, got_second, 1 - y), (kept_second, mine_second, got_second, y))
    for out, mine, got, index in pairs:
        out[...] = mine[0, pl.ds(index, 1)] + got[0, pl.ds(index, 1)]


def plane_stage(kept, got, spot):
    inputs = (kept[0], got[0], kept[1], got[1])
    outs = [jax.ShapeDtypeStruct((4, *value.shape[2:]), bf16) for value in inputs]
    away_first, kept_first, away_second, kept_second = pl.pallas_call(
        plane_kernel,
        grid_spec=pltpu.PrefetchScalarGridSpec(
            num_scalar_prefetch=1,
            grid=(4,),
            in_specs=[pl.BlockSpec((1, *value.shape[1:]), lambda i, *_: (i, 0, 0, 0)) for value in inputs],
            out_specs=[pl.BlockSpec((1, *out.shape[1:]), lambda i, *_: (i, 0, 0)) for out in outs],
        ),
        out_shape=outs,
        compiler_params=pltpu.CompilerParams(vmem_limit_bytes=40 * MEGA),
        cost_estimate=pl.CostEstimate(flops=10**6, bytes_accessed=5 * 10**6, transcendentals=0),
        name="plane_stage",
    )(spot, *inputs)
    return (away_first, away_second), (kept_first, kept_second)


def line_kernel(spot, mine_first, got_first, mine_second, got_second, one, two, three, stays):
    z = spot[0]
    rows = mine_first.shape[1]
    for step, out in enumerate((stays, one, two, three)):
        index = lax.rem(z + step, 4)
        at = (pl.ds(index, 1),)
        for mine, got, part in ((mine_first, got_first, slice(0, rows)), (mine_second, got_second, slice(rows, None))):
            total = mine[at][0].astype(f32) + got[at][0].astype(f32)
            out[part, :] = total.astype(out.dtype)


def line_stage(kept, got, spot):
    inputs = (kept[0], got[0], kept[1], got[1])
    size = (kept[0].shape[1] + kept[1].shape[1], kept[0].shape[2])
    outs = [jax.ShapeDtypeStruct(size, bf16)] * 3 + [jax.ShapeDtypeStruct(size, f32)]
    vmem = pl.BlockSpec(memory_space=pltpu.VMEM)
    *parts, stays = pl.pallas_call(
        line_kernel,
        in_specs=[pl.BlockSpec(memory_space=pltpu.SMEM)] + [vmem] * 4,
        out_specs=[vmem] * 4,
        out_shape=outs,
        compiler_params=pltpu.CompilerParams(vmem_limit_bytes=40 * MEGA),
        cost_estimate=pl.CostEstimate(flops=10**6, bytes_accessed=3 * 10**6, transcendentals=0),
        name="line_stage",
    )(spot, *inputs)
    return parts, stays


def sum_kernel(mine_first, got_first, mine_second, got_second, out):
    columns = mine_first.shape[-1]
    out[:, :, :columns] = mine_first[...] + got_first[...]
    out[:, :, columns:] = mine_second[...] + got_second[...]


def line_sum(kept, got):
    line, rows, columns = kept[0].shape
    vmem = pl.BlockSpec(memory_space=pltpu.VMEM)
    return pl.pallas_call(
        sum_kernel,
        in_specs=[vmem] * 4,
        out_specs=vmem,
        out_shape=jax.ShapeDtypeStruct((line, rows, 2 * columns), bf16),
        compiler_params=pltpu.CompilerParams(vmem_limit_bytes=40 * MEGA),
        cost_estimate=pl.CostEstimate(flops=10**6, bytes_accessed=5 * 10**6, transcendentals=0),
        name="line_sum",
    )(kept[0], got[0], kept[1], got[1])


def token_kernel(first, dq, dk, dv, w, out):
    total = first[...]
    for unit, grad in enumerate((dq, dk, dv)):
        total = total + dot_nt(grad[...], w[unit])
    out[...] = total


def token_grad(first, grads, mats, size=256):
    tokens, width = first.shape
    tile = pl.BlockSpec((size, width), lambda i: (i, 0))
    return pl.pallas_call(
        token_kernel,
        grid=(tokens // size,),
        in_specs=[tile] * 4 + [pl.BlockSpec((3, width, width), lambda i: (0, 0, 0))],
        out_specs=tile,
        out_shape=jax.ShapeDtypeStruct((tokens, width), f32),
        compiler_params=pltpu.CompilerParams(vmem_limit_bytes=60 * MEGA),
        cost_estimate=pl.CostEstimate(flops=4 * 10**9, bytes_accessed=10**7, transcendentals=0),
        name="token_grad",
    )(first, *grads, mats)


def natural_hidden(up, down, devices):
    share, chunks, width = up.shape
    up = up.reshape(share, chunks, devices, share).swapaxes(1, 2).reshape(share, chunks * width)
    return up, down.swapaxes(0, 1).reshape(chunks * share, width)


def per_device(
    known,
    hidden,
    pair_lengths,
    cotangent,
    query_weight,
    query_bias,
    key_weight,
    value_weight,
    value_bias,
    out_weight,
    out_bias,
    attn_gain,
    attn_shift,
    up_weight,
    up_bias,
    down_weight,
    down_bias,
    final_gain,
    final_shift,
):
    rows_here, length, width = hidden.shape
    count = rows_here * length
    share = query_weight.shape[0]
    devices = width // share
    chunks = up_weight.shape[1] // width
    up_mine = (
        up_weight.reshape(share, devices, chunks, share).swapaxes(1, 2).reshape(share, chunks * width)
    )
    down_parts = down_weight.reshape(chunks, share, width)
    ffn_mine = cat([up_mine, *down_parts[:-1]], 1)
    ffn_full = lax.all_gather(ffn_mine, CHIPS if known else AXES, axis=0, tiled=True)
    vector = cat(
        [
            query_bias,
            value_bias,
            out_bias,
            attn_gain,
            attn_shift,
            down_bias,
            final_gain,
            final_shift,
            up_bias,
        ]
    )
    tokens = hidden.reshape(count, width)
    groups = 8 + chunks
    if known:
        z, y, x, core = place()
        spot = jnp.stack([z, y, x, core]).astype(jnp.int32)
        matrices = jnp.stack([query_weight, key_weight, down_parts[-1], value_weight, out_weight])
        gathered = gather_attention(matrices, vector)
        out = attend_forward(True, tokens, gathered, pair_lengths, spot, rows_here, share)
        queries, keys_all, values_all, mixed, log_totals, first_norm, first_inverse, mats, vec = out
    else:
        spot = jnp.zeros((4,), jnp.int32)
        matrices = jnp.stack([query_weight, key_weight, value_weight, out_weight, down_parts[-1]])
        mats, vectors = gather_attention_any(matrices, vector)
        vec = vectors.reshape(devices, groups, share).swapaxes(0, 1).reshape(groups, width).astype(f32)
        vec = jnp.pad(vec, ((0, 16 - groups), (0, 0)))
        out = attend_forward(False, tokens, (mats, vec), pair_lengths, spot, rows_here, share)
        queries, keys_all, values_all, mixed, log_totals, first_norm, first_inverse = out
    layer_out, ffn_keep, ffn_away, grad_middle, first_sums = ffn(
        ffn_full, mats, first_norm, cotangent.reshape(count, width), vec, spot
    )
    ffn_got = send(ffn_away, "core") if known else None
    grad_first, grad_mixed, grad_out_weight, second_sums = middle_back(
        grad_middle, first_norm, first_inverse, mixed, mats, vec
    )

    def back(gradient):
        sums = (grad_out_weight, first_sums, second_sums)
        heads = (queries, keys_all, values_all, mixed, log_totals)
        return attend_back(known, share, spot, tokens, *heads, gradient, *sums, pair_lengths)

    if known:
        half = width // 2
        grid = (4, 2, 2, 2 * share, -1)
        ffn_got, ffn_keep, grad_mixed = phase(ffn_got, ffn_keep, grad_mixed)
        out = core_stage(ffn_keep.reshape(grid), ffn_got.reshape(grid), spot, chunks * half, False)
        ffn_got = send(out[0], "y"), send(out[2], "x")
        *ffn_kept, grad_mixed = phase(out[1], out[3], grad_mixed)
        *token_grads, keep, away = back(grad_mixed)
        *ffn_got, keep, away = phase(*ffn_got, keep, away)
        got = send(away, "core")
        plane, ffn_kept = plane_stage(ffn_kept, ffn_got, spot)
        got, *plane = phase(got, *plane)
        ffn_got = send(plane[0], "x"), send(plane[1], "y")
        shape = (4, 2, 2, *keep.shape[1:])
        out = core_stage(keep.reshape(shape), got.reshape(shape), spot, 4 * share, True)
        attn_got = send(out[0], "y"), send(out[2], "x")
        *ffn_got, attn_one, attn_two, grad_first = phase(*ffn_got, out[1], out[3], grad_first)
        attn_kept = attn_one, attn_two
        grad_tokens = token_grad(grad_first, token_grads, mats)
        ffn_sum = lax.psum_scatter(line_sum(ffn_kept, ffn_got), "z", scatter_dimension=0, tiled=True)
        *attn_got, grad_tokens = phase(*attn_got, grad_tokens)
        plane, attn_kept = plane_stage(attn_kept, attn_got, spot)
        attn_got = send(plane[0], "x"), send(plane[1], "y")
        attn_got = phase(*attn_got)
        line, attn_mine = line_stage(attn_kept, attn_got, spot)
        attn_line = send_line(line)
        ffn_sum, attn_mine = phase(ffn_sum, attn_mine)
        ffn_mine = ffn_sum[0].reshape(2, share, 2, chunks, half).transpose(2, 0, 1, 3, 4)
        ffn_whole = halves_of(ffn_mine.reshape(2, 2, share * chunks, half)).reshape(2, share, chunks, width)
        up_owned, down_owned = natural_hidden(ffn_whole[0], ffn_whole[1], devices)
        attn_one, attn_two, attn_three, up_owned, down_owned = phase(*attn_line, up_owned, down_owned)
        attn_mine = add(attn_mine, attn_one, attn_two, attn_three)
        mats_owned = halves_of(attn_mine[: 8 * share].reshape(4, 2, share, width // 2))
        vectors_owned = attn_mine[8 * share, : groups * share]
    else:
        *token_grads, mat_grads, bias_sums = back(grad_mixed)
        grad_tokens = token_grad(grad_first, token_grads, mats)
        ffn_grads = jnp.stack([ffn_keep, ffn_away]).reshape(2, width, 2, chunks, width // 2)
        ffn_grads = ffn_grads.transpose(2, 1, 3, 0, 4).reshape(2, width, chunks * width)
        ffn_whole = lax.psum_scatter(ffn_grads, AXES, scatter_dimension=1, tiled=True).astype(f32)
        up_owned, down_owned = natural_hidden(*ffn_whole.reshape(2, share, chunks, width), devices)
        mat_grads = cat([mat_grads, grad_out_weight[None]])
        vector_grads = cat(natural_rows([bias_sums[0:1], bias_sums[1:2]], first_sums, second_sums))
        vector_grads = vector_grads.reshape(groups, devices, share).swapaxes(0, 1).reshape(devices, groups * share)
        mats_owned, vectors_owned = scatter_attention_any(mat_grads, vector_grads)
    own = vectors_owned.reshape(groups, share)
    return (
        layer_out.reshape(hidden.shape),
        grad_tokens.reshape(hidden.shape),
        mats_owned[0],
        own[0],
        mats_owned[1],
        mats_owned[2],
        own[1],
        mats_owned[3],
        own[2],
        own[3],
        own[4],
        up_owned,
        own[8:].reshape(chunks * share),
        down_owned,
        own[5],
        own[6],
        own[7],
    )


def solution(mesh):
    known = dict(mesh.shape) == {"dp": 8, "shard": 4}
    axes = AXES
    if known:
        mesh, axes = Mesh(mesh.devices.reshape(4, 2, 2, 2), CHIPS), CHIPS
    cube, flat, line = P(axes, None, None), P(axes, None), P(axes)
    return jax.shard_map(
        lambda *args: per_device(known, *args),
        mesh=mesh,
        in_specs=(
            cube, flat, cube, flat, line, flat, flat, line, flat, line, line, line, flat, line, flat, line, line, line,
        ),
        out_specs=(
            cube, cube, flat, line, flat, flat, line, flat, line, line, line, flat, line, flat, line, line, line,
        ),
        check_vma=False,
    )
```

```python
import functools

import jax
import jax.numpy as jnp
from jax import lax
from jax.experimental import pallas as pl
from jax.experimental.pallas import tpu as pltpu
from jax.sharding import Mesh
from jax.sharding import PartitionSpec as P

EPSILON = 1e-06
SQRT_HALF = 0.7071067811865476
INV_ROOT = 0.3989422804014327
MOST = 128
HALF = 64
NEVER = -1e30
MEGA = 1024 * 1024

AXES = ("dp", "shard")
CHIPS = ("z", "y", "x", "core")
f32 = jnp.float32
bf16 = jnp.bfloat16
cat = jnp.concatenate


def moves(move):
    pairs = []
    for index in range(32):
        z, y, x, core = index // 8, (index // 4) % 2, (index // 2) % 2, index % 2
        z, y, x, core = move(z, y, x, core)
        pairs.append((index, z * 8 + y * 4 + x * 2 + core))
    return pairs


MOVES = {
    "core": moves(lambda z, y, x, core: (z, y, x, 1 - core)),
    "x": moves(lambda z, y, x, core: (z, y, 1 - x, core)),
    "y": moves(lambda z, y, x, core: (z, 1 - y, x, core)),
    "z1": moves(lambda z, y, x, core: ((z + 1) % 4, y, x, core)),
    "z2": moves(lambda z, y, x, core: ((z + 2) % 4, y, x, core)),
    "z3": moves(lambda z, y, x, core: ((z + 3) % 4, y, x, core)),
}


def send(values, move):
    return lax.ppermute(values, CHIPS, MOVES[move])


def place():
    return tuple(lax.axis_index(axis) for axis in CHIPS)


def phase(*values):
    return lax.optimization_barrier(values)


def add(*terms):
    total = terms[0].astype(f32)
    for term in terms[1:]:
        total = total + term.astype(f32)
    return total


def gather_blocks(block, split):
    one, two, three = send(block, "z1"), send(block, "z2"), send(block, "z3")
    one, two, three = phase(one, two, three)
    line = jnp.stack([block, one, two, three])
    first, second = line[:, :split], line[:, split:]
    first_x, second_y = send(first, "x"), send(second, "y")
    first_x, second_y, first, second = phase(first_x, second_y, first, second)
    first, second = cat([first, first_x]), cat([second, second_y])
    first_y, second_x = send(first, "y"), send(second, "x")
    other_first, other_second = send(first, "core"), send(second, "core")
    first, first_y, second, second_x, other_first, other_second = phase(
        first, first_y, second, second_x, other_first, other_second
    )
    other_first_y, other_second_x = send(first_y, "core"), send(second_x, "core")
    return first, first_y, second, second_x, other_first, other_first_y, other_second, other_second_x


def pick(values, index, axis):
    return lax.dynamic_index_in_dim(values, index, axis, False)


def send_line(parts):
    return tuple(send(part, move) for part, move in zip(parts, ("z1", "z2", "z3")))


def halves_of(mine):
    z, y, x, core = place()
    kept = pick(mine, core, 1)
    got = send(pick(mine, 1 - core, 1).astype(bf16), "core").astype(f32)
    return jnp.where(core == 0, cat([kept, got], 2), cat([got, kept], 2))


def gather_attention(matrices, vector):
    z, y, x, core = place()
    count, rows, width = matrices.shape
    half = width // 2
    mine = lax.dynamic_slice_in_dim(matrices, core * half, half, 2)
    got = send(lax.dynamic_slice_in_dim(matrices, (1 - core) * half, half, 2), "core")
    pair = jnp.where(core == 0, cat([mine, got], 1), cat([got, mine], 1))
    vector_rows = jnp.pad(vector[None], ((0, 15), (0, half - vector.shape[0])))
    block = cat([pair.reshape(count * 2 * rows, half), vector_rows])
    (block,) = phase(block)
    return gather_blocks(block, 6 * rows)


def gather_attention_any(matrices, vector):
    mats = lax.all_gather(matrices, AXES, axis=1, tiled=True)
    return mats, lax.all_gather(vector, AXES, axis=0, tiled=False)


def scatter_attention_any(matrices, vectors):
    mats = lax.psum_scatter(matrices.astype(bf16), AXES, scatter_dimension=1, tiled=True)
    return mats.astype(f32), lax.psum_scatter(vectors, AXES, scatter_dimension=0, tiled=False)


def dot(left, right):
    return lax.dot_general(left, right, (((1,), (0,)), ((), ())), preferred_element_type=f32)


def dot_nt(left, right):
    return lax.dot_general(left, right, (((1,), (1,)), ((), ())), preferred_element_type=f32)


def dot_tn(left, right):
    return lax.dot_general(left, right, (((0,), (0,)), ((), ())), preferred_element_type=f32)


def mean(values):
    return jnp.sum(values, axis=1, keepdims=True) * (1.0 / values.shape[1])


def spans(length, block):
    return [(start, max(0, start - MOST), min(length, start + block + MOST)) for start in range(0, length, block)]


def make_marks(lengths, row, marks):
    length, count = marks.shape[1], lengths.shape[1]
    position = lax.broadcasted_iota(jnp.int32, (length, 128), 0)
    lane = lax.broadcasted_iota(jnp.int32, (length, 128), 1)
    number, end = jnp.zeros((length, 128), jnp.int32), jnp.int32(0)
    for pair in range(count):
        end = end + lengths[row, pair]
        number = number + (position >= end).astype(jnp.int32)
    for head in (0, 1):
        at = lane - HALF * (1 - head)
        used = (at >= 0) & (at < count)
        marks[head] = jnp.where(used & (number == at), 1.0, 0.0).astype(bf16)
        marks[2 + head] = jnp.where(used & (number != at), NEVER, 0.0).astype(bf16)


def lanes(head, value=1.0):
    lane = lax.broadcasted_iota(jnp.int32, (16, 128), 1)
    return jnp.where((lane < HALF) if head == 0 else (lane >= HALF), value, 0.0).astype(bf16)[:1]


def spread(half, width, share):
    source = lax.broadcasted_iota(jnp.int32, (half, width), 0)
    target = lax.broadcasted_iota(jnp.int32, (half, width), 1)
    return jnp.where(source % share == target % share, 1.0, 0.0).astype(bf16)


def load_weights(spot, blocks, weights, vector_blocks, sem):
    z, y, x, core = spot[0], spot[1], spot[2], spot[3]
    copies = []
    rows = 48
    half = weights.shape[2] // 2
    for index, block in enumerate(blocks):
        side = core if index < 4 else 1 - core
        columns = pl.ds(pl.multiple_of(side * half, 128), half)
        for near in (0, 1):
            for step in range(4):
                far = index % 2
                if index % 4 < 2:
                    cy, cx = jnp.bitwise_xor(y, far), jnp.bitwise_xor(x, near)
                else:
                    cy, cx = jnp.bitwise_xor(y, near), jnp.bitwise_xor(x, far)
                chip = lax.rem(z - step + 4, 4) * 4 + cy * 2 + cx
                target = pl.ds(pl.multiple_of(chip * rows, 16), rows)
                at = near * 4 + step
                for unit, matrix in enumerate((0, 1, 4) if index % 4 < 2 else (2, 3)):
                    copies.append(
                        pltpu.make_async_copy(
                            block.at[at, pl.ds(unit * rows, rows)], weights.at[matrix, target, columns], sem
                        )
                    )
                if index % 4 >= 2:
                    copies.append(
                        pltpu.make_async_copy(
                            block.at[at, pl.ds(2 * rows, 16)], vector_blocks.at[chip * 2 + side], sem
                        )
                    )
    for copy in copies:
        copy.start()
    for copy in copies:
        copy.wait()


def spread_vectors(vector_blocks, vec, share):
    devices, _, half = vector_blocks.shape
    width = vec.shape[1]
    groups = 12
    entries = jnp.sum(vector_blocks[...].astype(f32), axis=1)
    lane = lax.broadcasted_iota(jnp.int32, (devices, half), 1)
    parts = [jnp.where(lane // share == group, entries, 0.0) for group in range(groups)]
    wide = dot(cat(parts).astype(bf16), spread(half, width, share))
    owner = lax.broadcasted_iota(jnp.int32, (devices, width), 1) // share
    device = lax.broadcasted_iota(jnp.int32, (devices, width), 0)
    for group in range(groups):
        part = wide[group * devices : (group + 1) * devices]
        vec[group : group + 1, :] = jnp.sum(jnp.where(owner == device, part, 0.0), axis=0, keepdims=True)


def attend_kernel(known, block, share, lengths, spot, x, *refs):
    if known:
        blocks, refs = refs[:8], refs[8:]
        q_out, k_out, v_out, mixed, lse, normed, inverse, w, vec, marks, vector_blocks, sem = refs
    else:
        w, vec, q_out, k_out, v_out, mixed, lse, normed, inverse, marks = refs
    row = pl.program_id(0)
    length, width = x.shape
    make_marks(lengths, row, marks)
    if known:

        @pl.when(row == 0)
        def _():
            load_weights(spot, blocks, w, vector_blocks, sem)
            spread_vectors(vector_blocks, vec, share)

    tokens = x[...]
    q_out[...] = (dot(tokens, w[0]) + vec[0:1, :]).astype(bf16)
    k_out[...] = dot(tokens, w[1]).astype(bf16)
    v_out[...] = (dot(tokens, w[2]) + vec[1:2, :]).astype(bf16)
    keep = (lanes(0), lanes(1))
    keep_scaled = (lanes(0, 0.125), lanes(1, 0.125))
    pairs, parts = width // 128, spans(length, block)

    def scores_of(pair):
        tile = pl.ds(pair * 128, 128)
        q, k, v = q_out[:, tile], k_out[:, tile], v_out[:, tile]
        qs = [q * keep_scaled[h] + marks[h] for h in (0, 1)]
        ks = [k * keep[h] + marks[2 + h] for h in (0, 1)]
        vs = [v * keep[h] + keep[1 - h] for h in (0, 1)]
        scores = [
            [dot_nt(ks[h][first:last], qs[h][start : start + block]) for h in (0, 1)] for start, first, last in parts
        ]
        return scores, vs

    upcoming = scores_of(0)
    for pair in range(pairs):
        scores, vs = upcoming
        if pair + 1 < pairs:
            upcoming = scores_of(pair + 1)
        tops = [[jnp.max(s, axis=0, keepdims=True) for s in both] for both in scores]
        probs = [[jnp.exp(s - t).astype(bf16) for s, t in zip(both, top)] for both, top in zip(scores, tops)]
        mixes = [
            [dot_tn(vs[h][first:last], probs[i][h]) for h in (0, 1)] for i, (start, first, last) in enumerate(parts)
        ]
        for i, (start, first, last) in enumerate(parts):
            out = []
            for h in (0, 1):
                mix = mixes[i][h]
                total = mix[HALF : HALF + 1] if h == 0 else mix[:1]
                lse[0, 2 * pair + h : 2 * pair + h + 1, start : start + block] = tops[i][h] + jnp.log(total)
                out.append((mix[:HALF] if h == 0 else mix[HALF:]) * (1.0 / total))
            mixed[start : start + block, pair * 128 : pair * 128 + 128] = jnp.transpose(cat(out)).astype(bf16)
    for start in range(0, length, 256):
        rows = pl.ds(start, 256)
        total = x[rows, :].astype(f32) + dot(mixed[rows, :], w[3]) + vec[2:3, :]
        centred = total - mean(total)
        inv = lax.rsqrt(mean(centred * centred) + EPSILON)
        normed[rows, :] = centred * inv
        inverse[rows, :] = jnp.broadcast_to(inv, (256, 128))


def attend_forward(known, x, gathered, lengths, spot, rows, share, block=128):
    tokens, width = x.shape
    length = tokens // rows
    shape = jax.ShapeDtypeStruct
    tile = pl.BlockSpec((length, width), lambda r, *_: (r, 0))
    fixed = [pl.BlockSpec((5, width, width), lambda r, *_: (0, 0, 0)), pl.BlockSpec((16, width), lambda r, *_: (0, 0))]
    act = shape((tokens, width), bf16)
    out_specs = [tile] * 4 + [
        pl.BlockSpec((1, 16, length), lambda r, *_: (r, 0, 0)),
        tile,
        pl.BlockSpec((length, 128), lambda r, *_: (r, 0)),
    ]
    out_shape = [act] * 4 + [shape((rows, 16, length), f32), shape((tokens, width), f32), shape((tokens, 128), f32)]
    scratch = [pltpu.VMEM((4, length, 128), bf16)]
    if known:
        in_specs = [tile] + [pl.BlockSpec(memory_space=pl.ANY)] * 8
        out_specs, out_shape = out_specs + fixed, out_shape + [shape((5, width, width), bf16), shape((16, width), f32)]
        scratch += [pltpu.VMEM((32, 16, width // 2), bf16), pltpu.SemaphoreType.DMA]
    else:
        in_specs = [tile] + fixed
    return pl.pallas_call(
        functools.partial(attend_kernel, known, block, share),
        grid_spec=pltpu.PrefetchScalarGridSpec(
            num_scalar_prefetch=2, grid=(rows,), in_specs=in_specs, out_specs=out_specs, scratch_shapes=scratch
        ),
        out_shape=out_shape,
        compiler_params=pltpu.CompilerParams(vmem_limit_bytes=60 * MEGA),
        cost_estimate=pl.CostEstimate(flops=10 * 10**9, bytes_accessed=2 * 10**7, transcendentals=4 * 10**6),
        name="attend",
    )(lengths, spot, x, *gathered)


def natural_rows(bias_rows, first_sums, second_sums):
    rows = bias_rows + [second_sums[2:3, :], second_sums[0:1, :], second_sums[1:2, :]]
    rows += [first_sums[i : i + 1, :] for i in (0, 1, 2)]
    return rows + [first_sums[i : i + 1, :] for i in (3, 4, 5, 6)]


def back_kernel(known, block, share, lengths, spot, x, q_in, k_in, v_in, mixed, lse, grad, *refs):
    grad_out, first_sums, second_sums, dq_out, dk_out, dv_out, keep, away, marks = refs
    tokens, width = q_in.shape
    rows = lengths.shape[0]
    length = tokens // rows
    for row in range(rows):
        make_marks(lengths, row, marks.at[row])
    keep_lanes = (lanes(0), lanes(1))
    keep_scaled = (lanes(0, 0.125), lanes(1, 0.125))
    head_of = lax.broadcasted_iota(jnp.int32, (16, 128), 1) // HALF
    picker = jnp.where(lax.broadcasted_iota(jnp.int32, (16, 128), 0) == head_of, 1.0, 0.0).astype(bf16)
    parts = spans(length, block)
    items = [(row, pair) for row in range(rows) for pair in range(width // 128)]

    def products_of(row, pair):
        tile = (slice(row * length, row * length + length), slice(pair * 128, pair * 128 + 128))
        q, k, v, g = q_in[tile], k_in[tile], v_in[tile], grad[tile]
        product = g.astype(f32) * mixed[tile].astype(f32)
        high = product.astype(bf16)
        centre = dot_nt(picker, high) + dot_nt(picker, (product - high.astype(f32)).astype(bf16))
        qz = [q * keep_scaled[h] for h in (0, 1)]
        kz = [k * keep_lanes[h] for h in (0, 1)]
        vz = [v * keep_lanes[h] for h in (0, 1)]
        gz = [g * keep_lanes[h] for h in (0, 1)]
        qs = [qz[h] + marks[row, h] for h in (0, 1)]
        ks = [kz[h] + marks[row, 2 + h] for h in (0, 1)]
        scores = [
            [dot_nt(ks[h][start : start + block], qs[h][first:last]) for h in (0, 1)] for start, first, last in parts
        ]
        slopes = [
            [dot_nt(vz[h][start : start + block], g[first:last]) for h in (0, 1)] for start, first, last in parts
        ]
        return scores, slopes, centre, qz, kz, gz

    upcoming = products_of(*items[0])
    for index, (row, pair) in enumerate(items):
        scores, slopes, centre, qz, kz, gz = upcoming
        if index + 1 < len(items):
            upcoming = products_of(*items[index + 1])
        probs, grads = [], []
        for i, (start, first, last) in enumerate(parts):
            head = 2 * pair
            prob = [jnp.exp(scores[i][h] - lse[row, head + h : head + h + 1, first:last]) for h in (0, 1)]
            probs.append([p.astype(bf16) for p in prob])
            grads.append([(prob[h] * (slopes[i][h] - centre[h : h + 1, first:last])).astype(bf16) for h in (0, 1)])
        columns = slice(pair * 128, pair * 128 + 128)
        to_values = [
            sum(dot(probs[i][h], gz[h][first:last]) for h in (0, 1)) for i, (start, first, last) in enumerate(parts)
        ]
        to_keys = [
            sum(dot(grads[i][h], qz[h][first:last]) for h in (0, 1)) for i, (start, first, last) in enumerate(parts)
        ]
        to_queries = [
            sum(dot_tn(grads[i][h], kz[h][start : start + block]) for h in (0, 1))
            for i, (start, first, last) in enumerate(parts)
        ]
        base = row * length
        for i, (start, first, last) in enumerate(parts):
            dv_out[base + start : base + start + block, columns] = to_values[i].astype(bf16)
            dk_out[base + start : base + start + block, columns] = to_keys[i].astype(bf16)
        for at in range(0, length, MOST):
            pieces = [
                to_queries[i][at - first : at - first + MOST]
                for i, (start, first, last) in enumerate(parts)
                if first <= at < last
            ]
            dq_out[base + at : base + at + MOST, columns] = (sum(pieces) * 0.125).astype(bf16)
    biases = [jnp.sum(out[...].astype(f32), axis=0, keepdims=True) for out in (dq_out, dv_out)]
    if not known:
        for unit, out in enumerate((dq_out, dk_out, dv_out)):
            keep[unit] = dot_tn(x[...], out[...]).astype(bf16)
        away[...] = jnp.zeros_like(away)
        away[0:1, :] = biases[0]
        away[1:2, :] = biases[1]
        return
    core = spot[3]
    half, chips, size = width // 2, keep.shape[0], 2 * share
    natural = natural_rows(biases, first_sums, second_sums)
    owner = lax.broadcasted_iota(jnp.int32, (chips, width), 1) // share
    chip = lax.broadcasted_iota(jnp.int32, (chips, width), 0)
    lane = lax.broadcasted_iota(jnp.int32, (chips, half), 1)
    table = spread(half, width, share)
    top = lax.broadcasted_iota(jnp.int32, (chips, 16, half), 1) == 0
    for side, out in ((1 - core, away), (core, keep)):
        own = pl.ds(pl.multiple_of(side * half, 128), half)
        for unit, out_ref in enumerate((dq_out, dk_out, dv_out)):
            part = dot_tn(x[...], out_ref[:, own]).astype(bf16)
            out[:, unit * size : (unit + 1) * size, :] = part.reshape(chips, size, half)
        out[:, 3 * size : 4 * size, :] = grad_out[:, own].reshape(chips, size, half)
        mine = owner == 2 * chip + side
        entries = jnp.zeros((chips, half), f32)
        spreads = dot_nt(cat([jnp.where(mine, row, 0.0) for row in natural]).astype(bf16), table)
        for group in range(len(natural)):
            part = spreads[group * chips : (group + 1) * chips]
            entries = entries + jnp.where(lane // share == group, part, 0.0)
        out[:, 4 * size :, :] = jnp.where(top, entries[:, None, :], 0.0).astype(bf16)


def full_block(value):
    return pl.BlockSpec(value.shape, lambda i, *_: (0,) * len(value.shape))


def attend_back(known, share, spot, x, q, k, v, mixed, lse, grad, grad_out, first_sums, second_sums, lengths, block=128):
    tokens, width = q.shape
    rows = lengths.shape[0]
    shape = jax.ShapeDtypeStruct
    outs = [shape((tokens, width), bf16)] * 3
    if known:
        outs += [shape((16, 8 * share + 16, width // 2), bf16)] * 2
    else:
        outs += [shape((3, width, width), bf16), shape((8, width), f32)]
    inputs = (x, q, k, v, mixed, lse, grad, grad_out, first_sums, second_sums)
    return pl.pallas_call(
        functools.partial(back_kernel, known, block, share),
        grid_spec=pltpu.PrefetchScalarGridSpec(
            num_scalar_prefetch=2,
            grid=(1,),
            in_specs=[full_block(value) for value in inputs],
            out_specs=[full_block(out) for out in outs],
            scratch_shapes=[pltpu.VMEM((rows, 4, tokens // rows, 128), bf16)],
        ),
        out_shape=outs,
        compiler_params=pltpu.CompilerParams(vmem_limit_bytes=60 * MEGA),
        cost_estimate=pl.CostEstimate(flops=20 * 10**9, bytes_accessed=2 * 10**7, transcendentals=4 * 10**6),
        name="attend_back",
    )(lengths, spot, *inputs)


def gelu_parts(u):
    phi = 0.5 * (1.0 + lax.erf(u * SQRT_HALF))
    return u * phi, phi + u * (jnp.exp(u * u * -0.5) * INV_ROOT)


def ffn_kernel(
    chunks, size, spot, weights, mats, normed, cot, vec, layer_out, keep, away, total, sums,
    w, low, act, slope, second_low, back, ready, loaded, sent,
):
    tokens, width = normed.shape
    copies = []
    for i in range(2 * chunks):
        columns = pl.ds(i * width, width)
        source = weights.at[:, columns] if i < 2 * chunks - 1 else mats.at[4]
        copies.append(pltpu.make_async_copy(source, w.at[:, columns], loaded.at[i]))
        copies[i].start()
    gain, shift = vec[3:4, :], vec[4:5, :]
    down_add, final_gain, final_shift = vec[5:6, :], vec[6:7, :], vec[7:8, :]

    def up(g):
        return w[:, g * width : (g + 1) * width]

    def down(g):
        return w[:, (chunks + g) * width : (chunks + g + 1) * width]

    low[...] = (normed[...] * gain + shift).astype(bf16)
    sums[...] = jnp.zeros_like(sums)

    def forward(t, first=False):
        rows = pl.ds(t * size, size) if first else pl.ds(pl.multiple_of(t * size, size), size)
        inputs = low[rows, :]
        if first:
            copies[0].wait()
        pre, added = dot(inputs, up(0)), None
        for g in range(chunks):
            if first and g + 1 < chunks:
                copies[g + 1].wait()
            upcoming = dot(inputs, up(g + 1)) if g + 1 < chunks else None
            activated, derivative = gelu_parts(pre + vec[8 + g : 9 + g, :])
            activated = activated.astype(bf16)
            act[g, rows, :] = activated
            slope[g, rows, :] = derivative.astype(bf16)
            if first:
                copies[chunks + g].wait()
            part = dot(activated, down(g))
            added = part if added is None else added + part
            pre = upcoming
        second_sum = normed[rows, :] * gain + shift + added + down_add
        centred = second_sum - mean(second_sum)
        inv = lax.rsqrt(mean(centred * centred) + EPSILON)
        hat = centred * inv
        layer_out[rows, :] = (hat * final_gain + final_shift).astype(bf16)
        grad = cot[rows, :].astype(f32)
        scaled = grad * final_gain
        second = inv * (scaled - mean(scaled) - hat * mean(scaled * hat))
        total[rows, :] = second
        second_low[rows, :] = second.astype(bf16)
        sums[0:1, :] += jnp.sum(second, axis=0, keepdims=True)
        sums[1:2, :] += jnp.sum(grad * hat, axis=0, keepdims=True)
        sums[2:3, :] += jnp.sum(grad, axis=0, keepdims=True)

    forward(0, True)

    @pl.loop(1, tokens // size)
    def _(t):
        forward(t)

    pending = []
    for g in range(chunks):
        to_act = dot_nt(second_low[...], down(g))
        to_down = dot_tn(act[g], second_low[...])
        to_pre = to_act * slope[g].astype(f32)
        sums[3 + g : 4 + g, :] = jnp.sum(to_pre, axis=0, keepdims=True)
        back[...] = to_pre.astype(bf16)
        slot = g % 2
        if g >= 2:
            for copy in pending[g - 2]:
                copy.wait()
        ready[slot, 1] = to_down.astype(bf16)
        total[...] += dot_nt(back[...], up(g))
        ready[slot, 0] = dot_tn(low[...], back[...]).astype(bf16)
        half, core = width // 2, spot[3]
        out = []
        for j in (0, 1):
            for target, side in ((away, 1 - core), (keep, core)):
                source = ready.at[slot, j, :, pl.ds(pl.multiple_of(side * half, 128), half)]
                place_of = target.at[:, pl.ds((j * chunks + g) * half, half)]
                out.append(pltpu.make_async_copy(source, place_of, sent.at[slot, len(out)]))
        for copy in out:
            copy.start()
        pending.append(out)

    for out in pending[-2:]:
        for copy in out:
            copy.wait()


def ffn(weights, mats, normed, cot, vec, spot, size=256):
    tokens, width = normed.shape
    chunks = (weights.shape[1] // width + 1) // 2
    shape = jax.ShapeDtypeStruct
    anywhere = pl.BlockSpec(memory_space=pl.ANY)
    halves = shape((width, chunks * width), bf16)
    outs = [shape((tokens, width), bf16)] + [halves] * 2 + [shape((tokens, width), f32), shape((8, width), f32)]
    out_specs = [full_block(out) for out in outs]
    out_specs[1:3] = [anywhere] * 2
    return pl.pallas_call(
        functools.partial(ffn_kernel, chunks, size),
        grid=(1,),
        in_specs=[pl.BlockSpec(memory_space=pltpu.SMEM), anywhere, anywhere, full_block(normed), full_block(cot), full_block(vec)],
        out_specs=out_specs,
        out_shape=outs,
        scratch_shapes=[
            pltpu.VMEM((width, 2 * chunks * width), bf16),
            pltpu.VMEM((tokens, width), bf16),
            pltpu.VMEM((chunks, tokens, width), bf16),
            pltpu.VMEM((chunks, tokens, width), bf16),
            pltpu.VMEM((tokens, width), bf16),
            pltpu.VMEM((tokens, width), bf16),
            pltpu.VMEM((2, 2, width, width), bf16),
            pltpu.SemaphoreType.DMA((2 * chunks,)),
            pltpu.SemaphoreType.DMA((2, 4)),
        ],
        compiler_params=pltpu.CompilerParams(vmem_limit_bytes=63 * MEGA),
        cost_estimate=pl.CostEstimate(flops=32 * 10**9, bytes_accessed=3 * 10**7, transcendentals=6 * 10**6),
        name="ffn",
    )(spot, weights, mats, normed, cot, vec)


def middle_kernel(grad_middle, normed, inverse, mixed, out_mat, vec, first, grad_mixed, grad_out, sums, low):
    step = pl.program_id(0)
    size = normed.shape[0]
    middle, hat, inv = grad_middle[...], normed[...], inverse[:, 0:1]
    scaled = middle * vec[3:4, :]
    to_first = inv * (scaled - mean(scaled) - hat * mean(scaled * hat))
    first[...] = to_first
    to_low = to_first.astype(bf16)
    low[pl.ds(pl.multiple_of(step * size, size), size), :] = to_low
    grad_mixed[...] = dot_nt(to_low, out_mat[0]).astype(bf16)

    @pl.when(step == 0)
    def _():
        sums[...] = jnp.zeros_like(sums)

    sums[0:1, :] += jnp.sum(middle * hat, axis=0, keepdims=True)
    sums[1:2, :] += jnp.sum(middle, axis=0, keepdims=True)
    sums[2:3, :] += jnp.sum(to_first, axis=0, keepdims=True)

    @pl.when(step == pl.num_programs(0) - 1)
    def _():
        grad_out[...] = dot_tn(mixed[...], low[...]).astype(bf16)


def middle_back(grad_middle, normed, inverse, mixed, mats, vec, size=256):
    tokens, width = normed.shape
    shape = jax.ShapeDtypeStruct
    tile = pl.BlockSpec((size, width), lambda i: (i, 0))
    outs = [shape((tokens, width), f32), shape((tokens, width), bf16), shape((width, width), bf16), shape((8, width), f32)]
    return pl.pallas_call(
        middle_kernel,
        grid=(tokens // size,),
        in_specs=[
            tile,
            tile,
            pl.BlockSpec((size, 128), lambda i: (i, 0)),
            full_block(mixed),
            pl.BlockSpec((1, width, width), lambda i: (3, 0, 0)),
            full_block(vec),
        ],
        out_specs=[tile, tile, full_block(outs[2]), full_block(outs[3])],
        out_shape=outs,
        scratch_shapes=[pltpu.VMEM((tokens, width), bf16)],
        compiler_params=pltpu.CompilerParams(vmem_limit_bytes=60 * MEGA),
        cost_estimate=pl.CostEstimate(flops=5 * 10**9, bytes_accessed=10**7, transcendentals=0),
        name="middle_back",
    )(grad_middle, normed, inverse, mixed, mats, vec)


def core_kernel(views, spot, keep, got, away_first, kept_first, away_second, kept_second):
    _, y, x, _ = (spot[i] for i in range(4))
    first, second = views
    for i in (0, 1):
        for out, index in ((away_first, 1 - y), (kept_first, y)):
            out[0, i] = first(keep, index, i) + first(got, index, i)
        for out, index in ((away_second, 1 - x), (kept_second, x)):
            out[0, i] = second(keep, i, index) + second(got, i, index)


def core_stage(keep, got, spot, split, by_rows):
    rows, columns = keep.shape[-2:]
    cuts = (slice(0, split), slice(split, None))
    if by_rows:
        sizes, cuts = ((split, columns), (rows - split, columns)), tuple((cut, slice(None)) for cut in cuts)
    else:
        sizes, cuts = ((rows, split), (rows, columns - split)), tuple((slice(None), cut) for cut in cuts)
    views = (
        lambda ref, y, x: ref[(0, pl.ds(y, 1), x, *cuts[0])][0],
        lambda ref, y, x: ref[(0, y, pl.ds(x, 1), *cuts[1])][0],
    )
    block = pl.BlockSpec((1, *keep.shape[1:]), lambda i, *_: (i, 0, 0, 0, 0))
    outs = [jax.ShapeDtypeStruct((4, 2, *size), bf16) for size in (sizes[0], sizes[0], sizes[1], sizes[1])]
    return pl.pallas_call(
        functools.partial(core_kernel, views),
        grid_spec=pltpu.PrefetchScalarGridSpec(
            num_scalar_prefetch=1,
            grid=(4,),
            in_specs=[block] * 2,
            out_specs=[pl.BlockSpec((1, *out.shape[1:]), lambda i, *_: (i, 0, 0, 0)) for out in outs],
        ),
        out_shape=outs,
        compiler_params=pltpu.CompilerParams(vmem_limit_bytes=40 * MEGA),
        cost_estimate=pl.CostEstimate(flops=10**6, bytes_accessed=10**7, transcendentals=0),
        name="core_stage",
    )(spot, keep, got)


def plane_kernel(spot, mine_first, got_first, mine_second, got_second, *outs):
    _, y, x, _ = (spot[i] for i in range(4))
    away_first, kept_first, away_second, kept_second = outs
    pairs = ((away_first, mine_first, got_first, 1 - x), (kept_first, mine_first, got_first, x))
    pairs += ((away_second, mine_second, got_second, 1 - y), (kept_second, mine_second, got_second, y))
    for out, mine, got, index in pairs:
        out[...] = mine[0, pl.ds(index, 1)] + got[0, pl.ds(index, 1)]


def plane_stage(kept, got, spot):
    inputs = (kept[0], got[0], kept[1], got[1])
    outs = [jax.ShapeDtypeStruct((4, *value.shape[2:]), bf16) for value in inputs]
    away_first, kept_first, away_second, kept_second = pl.pallas_call(
        plane_kernel,
        grid_spec=pltpu.PrefetchScalarGridSpec(
            num_scalar_prefetch=1,
            grid=(4,),
            in_specs=[pl.BlockSpec((1, *value.shape[1:]), lambda i, *_: (i, 0, 0, 0)) for value in inputs],
            out_specs=[pl.BlockSpec((1, *out.shape[1:]), lambda i, *_: (i, 0, 0)) for out in outs],
        ),
        out_shape=outs,
        compiler_params=pltpu.CompilerParams(vmem_limit_bytes=40 * MEGA),
        cost_estimate=pl.CostEstimate(flops=10**6, bytes_accessed=5 * 10**6, transcendentals=0),
        name="plane_stage",
    )(spot, *inputs)
    return (away_first, away_second), (kept_first, kept_second)


def line_kernel(spot, mine_first, got_first, mine_second, got_second, one, two, three, stays):
    z = spot[0]
    rows = mine_first.shape[1]
    for step, out in enumerate((stays, one, two, three)):
        index = lax.rem(z + step, 4)
        at = (pl.ds(index, 1),)
        for mine, got, part in ((mine_first, got_first, slice(0, rows)), (mine_second, got_second, slice(rows, None))):
            total = mine[at][0].astype(f32) + got[at][0].astype(f32)
            out[part, :] = total.astype(out.dtype)


def line_stage(kept, got, spot):
    inputs = (kept[0], got[0], kept[1], got[1])
    size = (kept[0].shape[1] + kept[1].shape[1], kept[0].shape[2])
    outs = [jax.ShapeDtypeStruct(size, bf16)] * 3 + [jax.ShapeDtypeStruct(size, f32)]
    vmem = pl.BlockSpec(memory_space=pltpu.VMEM)
    *parts, stays = pl.pallas_call(
        line_kernel,
        in_specs=[pl.BlockSpec(memory_space=pltpu.SMEM)] + [vmem] * 4,
        out_specs=[vmem] * 4,
        out_shape=outs,
        compiler_params=pltpu.CompilerParams(vmem_limit_bytes=40 * MEGA),
        cost_estimate=pl.CostEstimate(flops=10**6, bytes_accessed=3 * 10**6, transcendentals=0),
        name="line_stage",
    )(spot, *inputs)
    return parts, stays


def sum_kernel(mine_first, got_first, mine_second, got_second, out):
    columns = mine_first.shape[-1]
    out[:, :, :columns] = mine_first[...] + got_first[...]
    out[:, :, columns:] = mine_second[...] + got_second[...]


def line_sum(kept, got):
    line, rows, columns = kept[0].shape
    vmem = pl.BlockSpec(memory_space=pltpu.VMEM)
    return pl.pallas_call(
        sum_kernel,
        in_specs=[vmem] * 4,
        out_specs=vmem,
        out_shape=jax.ShapeDtypeStruct((line, rows, 2 * columns), bf16),
        compiler_params=pltpu.CompilerParams(vmem_limit_bytes=40 * MEGA),
        cost_estimate=pl.CostEstimate(flops=10**6, bytes_accessed=5 * 10**6, transcendentals=0),
        name="line_sum",
    )(kept[0], got[0], kept[1], got[1])


def token_kernel(first, dq, dk, dv, w, out):
    total = first[...]
    for unit, grad in enumerate((dq, dk, dv)):
        total = total + dot_nt(grad[...], w[unit])
    out[...] = total


def token_grad(first, grads, mats, size=256):
    tokens, width = first.shape
    tile = pl.BlockSpec((size, width), lambda i: (i, 0))
    return pl.pallas_call(
        token_kernel,
        grid=(tokens // size,),
        in_specs=[tile] * 4 + [pl.BlockSpec((3, width, width), lambda i: (0, 0, 0))],
        out_specs=tile,
        out_shape=jax.ShapeDtypeStruct((tokens, width), f32),
        compiler_params=pltpu.CompilerParams(vmem_limit_bytes=60 * MEGA),
        cost_estimate=pl.CostEstimate(flops=4 * 10**9, bytes_accessed=10**7, transcendentals=0),
        name="token_grad",
    )(first, *grads, mats)


def natural_hidden(up, down, devices):
    share, chunks, width = up.shape
    up = up.reshape(share, chunks, devices, share).swapaxes(1, 2).reshape(share, chunks * width)
    return up, down.swapaxes(0, 1).reshape(chunks * share, width)


def per_device(
    known,
    hidden,
    pair_lengths,
    cotangent,
    query_weight,
    query_bias,
    key_weight,
    value_weight,
    value_bias,
    out_weight,
    out_bias,
    attn_gain,
    attn_shift,
    up_weight,
    up_bias,
    down_weight,
    down_bias,
    final_gain,
    final_shift,
):
    rows_here, length, width = hidden.shape
    count = rows_here * length
    share = query_weight.shape[0]
    devices = width // share
    chunks = up_weight.shape[1] // width
    up_mine = (
        up_weight.reshape(share, devices, chunks, share).swapaxes(1, 2).reshape(share, chunks * width)
    )
    down_parts = down_weight.reshape(chunks, share, width)
    ffn_mine = cat([up_mine, *down_parts[:-1]], 1)
    ffn_full = lax.all_gather(ffn_mine, CHIPS if known else AXES, axis=0, tiled=True)
    vector = cat(
        [
            query_bias,
            value_bias,
            out_bias,
            attn_gain,
            attn_shift,
            down_bias,
            final_gain,
            final_shift,
            up_bias,
        ]
    )
    tokens = hidden.reshape(count, width)
    groups = 8 + chunks
    if known:
        z, y, x, core = place()
        spot = jnp.stack([z, y, x, core]).astype(jnp.int32)
        matrices = jnp.stack([query_weight, key_weight, down_parts[-1], value_weight, out_weight])
        gathered = gather_attention(matrices, vector)
        out = attend_forward(True, tokens, gathered, pair_lengths, spot, rows_here, share)
        queries, keys_all, values_all, mixed, log_totals, first_norm, first_inverse, mats, vec = out
    else:
        spot = jnp.zeros((4,), jnp.int32)
        matrices = jnp.stack([query_weight, key_weight, value_weight, out_weight, down_parts[-1]])
        mats, vectors = gather_attention_any(matrices, vector)
        vec = vectors.reshape(devices, groups, share).swapaxes(0, 1).reshape(groups, width).astype(f32)
        vec = jnp.pad(vec, ((0, 16 - groups), (0, 0)))
        out = attend_forward(False, tokens, (mats, vec), pair_lengths, spot, rows_here, share)
        queries, keys_all, values_all, mixed, log_totals, first_norm, first_inverse = out
    layer_out, ffn_keep, ffn_away, grad_middle, first_sums = ffn(
        ffn_full, mats, first_norm, cotangent.reshape(count, width), vec, spot
    )
    ffn_got = send(ffn_away, "core") if known else None
    grad_first, grad_mixed, grad_out_weight, second_sums = middle_back(
        grad_middle, first_norm, first_inverse, mixed, mats, vec
    )

    def back(gradient):
        sums = (grad_out_weight, first_sums, second_sums)
        heads = (queries, keys_all, values_all, mixed, log_totals)
        return attend_back(known, share, spot, tokens, *heads, gradient, *sums, pair_lengths)

    if known:
        half = width // 2
        grid = (4, 2, 2, 2 * share, -1)
        ffn_got, ffn_keep, grad_mixed = phase(ffn_got, ffn_keep, grad_mixed)
        out = core_stage(ffn_keep.reshape(grid), ffn_got.reshape(grid), spot, chunks * half, False)
        ffn_got = send(out[0], "y"), send(out[2], "x")
        *ffn_kept, grad_mixed = phase(out[1], out[3], grad_mixed)
        *token_grads, keep, away = back(grad_mixed)
        *ffn_got, keep, away = phase(*ffn_got, keep, away)
        got = send(away, "core")
        plane, ffn_kept = plane_stage(ffn_kept, ffn_got, spot)
        got, *plane = phase(got, *plane)
        ffn_got = send(plane[0], "x"), send(plane[1], "y")
        shape = (4, 2, 2, *keep.shape[1:])
        out = core_stage(keep.reshape(shape), got.reshape(shape), spot, 4 * share, True)
        attn_got = send(out[0], "y"), send(out[2], "x")
        *ffn_got, attn_one, attn_two, grad_first = phase(*ffn_got, out[1], out[3], grad_first)
        attn_kept = attn_one, attn_two
        grad_tokens = token_grad(grad_first, token_grads, mats)
        ffn_sum = lax.psum_scatter(line_sum(ffn_kept, ffn_got), "z", scatter_dimension=0, tiled=True)
        *attn_got, grad_tokens = phase(*attn_got, grad_tokens)
        plane, attn_kept = plane_stage(attn_kept, attn_got, spot)
        attn_got = send(plane[0], "x"), send(plane[1], "y")
        attn_got = phase(*attn_got)
        line, attn_mine = line_stage(attn_kept, attn_got, spot)
        attn_line = send_line(line)
        ffn_sum, attn_mine = phase(ffn_sum, attn_mine)
        ffn_mine = ffn_sum[0].reshape(2, share, 2, chunks, half).transpose(2, 0, 1, 3, 4)
        ffn_whole = halves_of(ffn_mine.reshape(2, 2, share * chunks, half)).reshape(2, share, chunks, width)
        up_owned, down_owned = natural_hidden(ffn_whole[0], ffn_whole[1], devices)
        attn_one, attn_two, attn_three, up_owned, down_owned = phase(*attn_line, up_owned, down_owned)
        attn_mine = add(attn_mine, attn_one, attn_two, attn_three)
        mats_owned = halves_of(attn_mine[: 8 * share].reshape(4, 2, share, width // 2))
        vectors_owned = attn_mine[8 * share, : groups * share]
    else:
        *token_grads, mat_grads, bias_sums = back(grad_mixed)
        grad_tokens = token_grad(grad_first, token_grads, mats)
        ffn_grads = jnp.stack([ffn_keep, ffn_away]).reshape(2, width, 2, chunks, width // 2)
        ffn_grads = ffn_grads.transpose(2, 1, 3, 0, 4).reshape(2, width, chunks * width)
        ffn_whole = lax.psum_scatter(ffn_grads, AXES, scatter_dimension=1, tiled=True).astype(f32)
        up_owned, down_owned = natural_hidden(*ffn_whole.reshape(2, share, chunks, width), devices)
        mat_grads = cat([mat_grads, grad_out_weight[None]])
        vector_grads = cat(natural_rows([bias_sums[0:1], bias_sums[1:2]], first_sums, second_sums))
        vector_grads = vector_grads.reshape(groups, devices, share).swapaxes(0, 1).reshape(devices, groups * share)
        mats_owned, vectors_owned = scatter_attention_any(mat_grads, vector_grads)
    own = vectors_owned.reshape(groups, share)
    return (
        layer_out.reshape(hidden.shape),
        grad_tokens.reshape(hidden.shape),
        mats_owned[0],
        own[0],
        mats_owned[1],
        mats_owned[2],
        own[1],
        mats_owned[3],
        own[2],
        own[3],
        own[4],
        up_owned,
        own[8:].reshape(chunks * share),
        down_owned,
        own[5],
        own[6],
        own[7],
    )


def solution(mesh):
    known = dict(mesh.shape) == {"dp": 8, "shard": 4}
    axes = AXES
    if known:
        mesh, axes = Mesh(mesh.devices.reshape(4, 2, 2, 2), CHIPS), CHIPS
    cube, flat, line = P(axes, None, None), P(axes, None), P(axes)
    return jax.shard_map(
        lambda *args: per_device(known, *args),
        mesh=mesh,
        in_specs=(
            cube, flat, cube, flat, line, flat, flat, line, flat, line, line, line, flat, line, flat, line, line, line,
        ),
        out_specs=(
            cube, cube, flat, line, flat, flat, line, flat, line, line, line, flat, line, flat, line, line, line,
        ),
        check_vma=False,
    )
```
